128 devices in a mesh: outer: 2 (over z_hi), inner: 64 (over z_lo, y, x, core).
Axes of the slice: x: 4, y: 4, z: 4 (z_hi: 2, z_lo: 2; z = z_hi * 2 + z_lo), core: 2. Of those that a mesh axis runs over, the one named last changes fastest.
Arguments:
- grad_out: bfloat16 [32768, 3584], P(('outer', 'inner')), may hold values from -6 to 6
- gates: bfloat16 [32768, 4], P(('outer', 'inner')), may hold values from 0.049804688 to 1
- routes: int32 [32768, 4], P(('outer', 'inner')), may hold values from 0 to 127, all different within a row; in each aligned block of 256 rows (0 to 255, 256 to 511, ...) at most 10 rows name the same one
- w_down: bfloat16 [128, 1024, 3584], P('inner', 'outer'), may hold values from -0.1875 to 0.1875
- saved_hidden: bfloat16 [128, 1280, 1024], P('inner', None, 'outer'), may hold values from -0.59765625 to 0.59765625
Outputs:
- d_gates: float32 [32768, 4], P(('outer', 'inner'))
- d_down: bfloat16 [128, 1024, 3584], P('inner', 'outer')
- d_hidden: bfloat16 [128, 1280, 1024], P('inner', None, 'outer')
The draws below stay inside these ranges and needn't reach their ends.
Inputs may be any that keep to these rules, and one draw needn't show every extreme that they name: `routes`: in the 256 rows of one device no expert is named by more than 10 slots, a bound that some block reaches.
All inputs are finite; a program needn't handle non-finite values.
Results may differ from the reference program's by a relative error of at most 0.0049.
Values may be sent and summed in bfloat16 or wider, within the bound.
No kernel may reach another device: no remote copies, remote signals or barrier semaphores. Data moves between devices by JAX's collectives and lax.ppermute only.
A program may use at most 128 MiB of HBM per device.

```python
import math
import jax
import jax.numpy as jnp
import numpy as np
from jax import lax

TOK_DEV = 256
D = 3584
FF = 1024
TOP = 4
TOKENS = 32768
EXPERTS = 128
CAP = 10
N_OUTER = 2
N_INNER = 64


def block_scale(stream_key, shape, cuts, least, largest):
    def one(axis_at, parts):
        draws = jax.random.uniform(jax.random.fold_in(jax.random.fold_in(stream_key, 6), axis_at), (parts,), jnp.float32, least / len(cuts), largest / len(cuts))
        return jnp.repeat(jnp.exp(draws), shape[axis_at] // parts).reshape((-1,) + (1,) * (len(shape) - axis_at - 1))

    loudness = one(*cuts[0])
    for cut in cuts[1:]:
        loudness = loudness * one(*cut)
    return loudness


def deal_out(own_key, own, number, rows, count, top, limit, slope):
    sequence = jax.random.permutation(own_key, count)
    packed, ordinary = portions_of(count, rows * top, limit, slope, True), portions_of(count, rows * top, limit, slope, False)
    places = jnp.arange(count)

    def named(lengths, turn):
        used = int((lengths > 0).sum())
        fixed = max(1, used // 4)
        shifted = fixed + (places - fixed + turn * (used - fixed)) % max(1, count - fixed)
        return jnp.zeros((count,), jnp.int32).at[sequence[jnp.where(places < fixed, places, shifted)]].set(jnp.asarray(lengths, jnp.int32))

    lengths = jnp.where(number % 4 == 0, named(packed, number // 4), named(ordinary, number - number // 4 - 1))
    mixed = jax.random.permutation(jax.random.fold_in(own, 3), count)
    donor, sink = mixed[0:count // 2 * 2:2], mixed[1:count // 2 * 2:2]
    room = jnp.minimum(lengths[donor] - 1, limit - lengths[sink]) // 2
    room = jnp.where((donor == sequence[0]) | (sink == sequence[0]) | (lengths[sink] == 0), 0, jnp.maximum(room, 0))
    shifted = jax.random.randint(jax.random.fold_in(own, 4), (count // 2,), 0, 1 << 20) % (room + 1)
    lengths = lengths.at[donor].add(-shifted).at[sink].add(shifted)
    members = jnp.searchsorted(jnp.cumsum(lengths), jnp.arange(rows * top), side="right").astype(jnp.int32)
    grid = members.reshape(top, rows).T
    grid = grid[jax.random.permutation(jax.random.fold_in(own, 1), rows)]
    turn = jax.random.randint(jax.random.fold_in(own, 2), (rows, 1), 0, top)
    return jnp.take_along_axis(grid, (jnp.arange(top)[None, :] + turn) % top, axis=1)


def portions_of(amount, total, bound, lean, full):
    portions = [(1 << 20) // math.isqrt(rank ** lean) + 1 for rank in range(1, amount + 1)]
    largest = bound if full else min(bound, max(-(-total // amount), total * portions[0] // sum(portions)))
    least = 1 if total - largest >= amount - 1 else 0
    counts, spare = [largest] + [least] * (amount - 1), total - largest - least * (amount - 1)
    while spare > 0:
        free = [i for i in range(1, amount) if counts[i] < largest] or [i for i in range(1, amount) if counts[i] < bound]
        pool, left = sum([portions[i] for i in free]), spare
        for i in free:
            more = min(bound - counts[i], max(1, left * portions[i] // pool), spare)
            counts[i] = counts[i] + more
            spare = spare - more
    return np.array(counts)


def normal_values(key, extent, width, bound, cuts=(), kind=jnp.bfloat16):
    drawn = jax.random.normal(key, extent, jnp.float32) * width
    if len(cuts) > 0:
        drawn = block_scale(key, extent, cuts, -0.22, 0.18) * drawn
    return jnp.clip(drawn, min=-bound, max=bound).astype(kind)


def setup_inputs(seed: int = 0) -> dict:
    key_list = jax.random.split(jax.random.key(seed), 6)
    grad_out = normal_values(key_list[0], (TOKENS, D), 1.0, 6.0, ((0, 128),))
    gates = jnp.clip(jnp.exp(math.log(1.0) - 2.9996462 * jax.random.uniform(key_list[1], (TOKENS, TOP), jnp.float32) ** block_scale(key_list[1], (TOKENS, TOP), ((0, 128),), -0.2, 0.2)), 0.049804688, 1.0).astype(jnp.bfloat16)
    routes_keys = jax.random.split(jax.random.fold_in(key_list[2], 1), TOKENS // TOK_DEV)
    routes_turns = jax.random.permutation(jax.random.fold_in(key_list[2], 3), TOKENS // TOK_DEV)
    routes = jax.vmap(lambda own, number: deal_out(jax.random.fold_in(key_list[2], 2), own, number, TOK_DEV, EXPERTS, TOP, CAP, 2))(routes_keys, routes_turns).reshape((TOKENS, TOP))
    w_down = normal_values(key_list[3], (EXPERTS, FF, D), FF ** -0.5, 0.1875, ((0, 64), (1, 2)))
    saved_hidden = normal_values(key_list[4], (EXPERTS, N_OUTER * N_INNER * CAP, FF), 0.1, 0.59765625, ((0, 64), (2, 2)))
    return {"grad_out": grad_out, "gates": gates, "routes": routes, "w_down": w_down, "saved_hidden": saved_hidden}


def route_rows(routes):
    flat_routes = routes.reshape(-1)
    slot_count = flat_routes.shape[0]
    per_source = TOK_DEV * TOP
    onehot = (flat_routes[:, None] == jnp.arange(EXPERTS, dtype=jnp.int32)[None, :]).astype(jnp.int32)
    grouped = onehot.reshape(slot_count // per_source, per_source, EXPERTS)
    earlier = jnp.cumsum(grouped, axis=1) - grouped
    position = jnp.sum(earlier * grouped, axis=2).reshape(-1)
    source = jnp.arange(slot_count, dtype=jnp.int32) // per_source
    return flat_routes, source * CAP + position


def reference(grad_out, gates, routes, w_down, saved_hidden):
    expert_ids, row_ids = route_rows(routes)
    slot_count = expert_ids.shape[0]
    row_total = N_OUTER * N_INNER * CAP
    token_ids = jnp.arange(slot_count, dtype=jnp.int32) // TOP
    token_at = jnp.zeros((EXPERTS, row_total), jnp.int32).at[expert_ids, row_ids].set(token_ids)
    filled = jnp.zeros((EXPERTS, row_total), jnp.int32).at[expert_ids, row_ids].set(1)
    gate_at = jnp.zeros((EXPERTS, row_total), jnp.float32).at[expert_ids, row_ids].set(
        gates.reshape(-1).astype(jnp.float32))

    def per_expert(pieces):
        token_row, filled_row, gate_row, weight, hidden = pieces
        routed = jnp.where(filled_row[:, None] > 0, grad_out[token_row], jnp.zeros((), grad_out.dtype))
        backward = jnp.dot(routed, weight.T, preferred_element_type=jnp.float32)
        d_hidden = (gate_row[:, None] * backward).astype(jnp.bfloat16)
        scaled = (gate_row[:, None] * routed.astype(jnp.float32)).astype(jnp.bfloat16)
        d_weight = jnp.dot(hidden.T, scaled, preferred_element_type=jnp.float32).astype(jnp.bfloat16)
        gate_terms = jnp.sum(hidden.astype(jnp.float32) * backward, axis=1)
        return d_weight, d_hidden, gate_terms

    d_down, d_hidden, gate_terms = lax.map(per_expert, (token_at, filled, gate_at, w_down, saved_hidden))
    d_gates = gate_terms[expert_ids, row_ids].reshape(TOKENS, TOP)
    return d_gates, d_down, d_hidden
```

```python
import jax
import jax.numpy as jnp
from jax import lax
from jax.sharding import Mesh, PartitionSpec as P

Z = ("zh", "zl")
PLANE = ("y", "x", "core")
ALL = ("zh", "zl", "y", "x", "core")
CAP = 10
BF = jnp.bfloat16
F32 = jnp.float32


def z_shift(value, step):
    return lax.ppermute(value, Z, [(i, (i + step) % 4) for i in range(4)])


def core_swap(value):
    return lax.ppermute(value, "core", [(0, 1), (1, 0)])


def picker(row_ids, rows):
    wanted = jnp.arange(rows, dtype=jnp.int32)[:, None]
    hit = row_ids[0][None, :] == wanted
    for k in range(1, row_ids.shape[0]):
        hit = hit | (row_ids[k][None, :] == wanted)
    return hit.astype(BF)


def dot(a, b, out=F32):
    return jnp.dot(a, b, preferred_element_type=F32).astype(out)


def shards(grad_out, gates, routes, w_down, saved_hidden):
    tokens, width = grad_out.shape
    zh, zl = lax.axis_index("zh"), lax.axis_index("zl")
    core = lax.axis_index("core")
    z = zh * 2 + zl
    inner = ((zl * 4 + lax.axis_index("y")) * 4 + lax.axis_index("x")) * 2 + core
    experts = 128
    hidden = w_down.shape[1]

    from_up = z_shift(grad_out, -1)
    from_down = z_shift(grad_out, 1)
    half = width // 2
    far = jnp.concatenate(
        [z_shift(from_down[:, :half], 1), z_shift(from_up[:, half:], -1)], axis=1
    )
    other = core_swap(grad_out)

    r = routes.T
    names = jnp.arange(experts, dtype=jnp.int32)
    onehot = routes[:, :, None] == names[None, None, :]
    named = jnp.any(onehot, axis=1).astype(BF)
    order = jnp.arange(tokens, dtype=jnp.int32)
    earlier = dot((order[:, None] > order[None, :]).astype(BF), named)
    pos = jnp.sum(jnp.where(onehot, earlier[:, None, :], 0.0), axis=2).astype(jnp.int32).T
    code = r * 16 + pos
    code_other = core_swap(code)

    def fields(c):
        pos, route = c % 16, c // 16
        e, dcore, yx, dzl = route % 2, (route // 2) % 2, (route // 4) % 16, route // 64
        return pos, e, dcore, yx, dzl

    def ids1(c, csrc):
        pos, e, dcore, yx, dzl = fields(c)
        return jnp.where((e == 1) & (dcore == core), yx * 40 + dzl * 20 + csrc * 10 + pos, -1)

    pick1 = picker(jnp.concatenate([ids1(code, core), ids1(code_other, 1 - core)], axis=1), 640)
    send1 = dot(pick1, jnp.concatenate([grad_out, other], axis=0), BF).reshape(16, 40, width)
    got1 = lax.all_to_all(send1, ("y", "x"), 0, 0, tiled=True).reshape(640, width)
    out_row = jnp.arange(320, dtype=jnp.int32)
    at_row = (out_row // 20) * 40 + out_row % 20
    source_row = jnp.arange(640, dtype=jnp.int32)[None, :]
    own = dot((source_row == (at_row + zl * 20)[:, None]).astype(BF), got1, BF)
    away = dot((source_row == (at_row + (1 - zl) * 20)[:, None]).astype(BF), got1, BF)
    rows1 = jnp.concatenate([own, z_shift(away, 1), z_shift(own, 2), z_shift(away, -1)], axis=0)

    codes = [code, z_shift(code, 1), z_shift(code, 2), z_shift(code, -1)]

    def ids0(c, zsrc):
        pos, e, dcore, yx, dzl = fields(c)
        return jnp.where((e == 0) & (dzl == zl), (yx * 2 + dcore) * 40 + zsrc * 10 + pos, -1)

    pick0 = picker(
        jnp.concatenate([ids0(c, (z - k) % 4) for k, c in enumerate(codes)], axis=1), 1280
    )
    line = jnp.concatenate([grad_out, from_down, far, from_up], axis=0)
    send0 = dot(pick0, line, BF).reshape(32, 40, width)
    rows0 = lax.all_to_all(send0, PLANE, 0, 0, tiled=True).reshape(1280, width)

    table = r * CAP + pos
    gate_table = jnp.sum(
        jnp.where(
            table.reshape(1, -1) == jnp.arange(experts * CAP, dtype=jnp.int32)[:, None],
            gates.T.reshape(1, -1).astype(F32),
            0.0,
        ),
        axis=1,
    ).astype(BF)
    all_gates = lax.all_gather(gate_table[None], ALL, axis=0, tiled=True)
    my_gates = lax.dynamic_slice(all_gates, (0, inner * 20), (128, 20)).astype(F32)

    def to0(a):
        return a.reshape(4, 32, CAP, -1).transpose(1, 0, 2, 3).reshape(1280, -1)

    def from0(a):
        return a.reshape(32, 4, CAP, -1).transpose(1, 0, 2, 3).reshape(1280, -1)

    def to1(a):
        a = a.reshape(4, 320, -1)
        return jnp.concatenate(
            [lax.dynamic_index_in_dim(a, (z - k) % 4, 0, False) for k in range(4)], axis=0
        )

    def from1(a):
        a = a.reshape(4, 320, -1)
        return jnp.concatenate(
            [lax.dynamic_index_in_dim(a, (z - i) % 4, 0, False) for i in range(4)], axis=0
        )

    def expert(rows, weight, saved, gate):
        back = lax.dot_general(rows, weight, (((1,), (1,)), ((), ())), preferred_element_type=F32)
        d_hidden = (gate * back).astype(BF)
        scaled = (gate * rows.astype(F32)).astype(BF)
        d_down = lax.dot_general(
            saved, scaled, (((0,), (0,)), ((), ())), preferred_element_type=F32
        ).astype(BF)
        terms = jnp.sum(saved.astype(F32) * back, axis=1, keepdims=True)
        return d_hidden, d_down, terms

    gate0 = to0(my_gates[:, :CAP].reshape(1280, 1))
    gate1 = to1(my_gates[:, CAP:].reshape(1280, 1))
    dh0, dd0, terms0 = expert(rows0, w_down[0], to0(saved_hidden[0]), gate0)
    dh1, dd1, terms1 = expert(rows1, w_down[1], to1(saved_hidden[1]), gate1)
    d_hidden = jnp.stack([from0(dh0), from1(dh1)])
    d_down = jnp.stack([dd0, dd1])

    terms = jnp.concatenate(
        [from0(terms0).reshape(128, CAP), from1(terms1).reshape(128, CAP)], axis=1
    )
    returned = lax.all_to_all(terms, ALL, 0, 0, tiled=True)
    returned = (returned[:64] + returned[64:]).reshape(-1)
    d_gates = jnp.sum(
        jnp.where(
            table.reshape(1, -1) == jnp.arange(experts * CAP, dtype=jnp.int32)[:, None],
            returned[:, None],
            0.0,
        ),
        axis=0,
    ).reshape(4, tokens).T
    return d_gates, d_down, d_hidden


def solution(mesh):
    fine = Mesh(mesh.devices.reshape(2, 2, 4, 4, 2), ALL)
    in_specs = (
        P(ALL, None),
        P(ALL, None),
        P(ALL, None),
        P(("zl", "y", "x", "core"), "zh", None),
        P(("zl", "y", "x", "core"), None, "zh"),
    )
    out_specs = (P(ALL, None), in_specs[3], in_specs[4])
    return jax.shard_map(shards, mesh=fine, in_specs=in_specs, out_specs=out_specs, check_vma=False)
```

```python
import functools

import jax
import jax.numpy as jnp
from jax import lax
from jax.experimental import pallas as pl
from jax.experimental.pallas import tpu as pltpu
from jax.sharding import Mesh, PartitionSpec as P

Z = ("zh", "zl")
PLANE = ("y", "x", "core")
ALL = ("zh", "zl", "y", "x", "core")
CAP = 10
TOP = 4
EXPERTS = 128
BF = jnp.bfloat16
F32 = jnp.float32
I32 = jnp.int32
PARAMS = dict(vmem_limit_bytes=48 * 1024 * 1024)


def z_shift(value, step):
    return lax.ppermute(value, Z, [(i, (i + step) % 4) for i in range(4)])


def core_swap(value):
    return lax.ppermute(value, "core", [(0, 1), (1, 0)])


def dot(a, b):
    return jnp.dot(a, b, preferred_element_type=F32)


def cost(flops, nbytes):
    return pl.CostEstimate(flops=int(flops), bytes_accessed=int(nbytes), transcendentals=0)


def positions(meta):
    tokens = meta.shape[1]
    names = lax.broadcasted_iota(I32, (EXPERTS, tokens), 0)
    routes = [meta[k : k + 1, :].astype(I32) for k in range(TOP)]
    hits = [names == r for r in routes]
    named = sum(h.astype(F32) for h in hits)
    first = lax.broadcasted_iota(I32, (tokens, tokens), 0)
    second = lax.broadcasted_iota(I32, (tokens, tokens), 1)
    earlier = dot(named.astype(BF), (first < second).astype(F32).astype(BF))
    places = [
        jnp.sum(jnp.where(h, earlier, 0.0), axis=0, keepdims=True).astype(I32) for h in hits
    ]
    return routes, places


def pick_kernel(sources, expert, where, scalars, *refs):
    metas, tokens = refs[:sources], refs[sources : 2 * sources]
    out, picker = refs[2 * sources], refs[2 * sources + 1]
    rows = picker.shape[0]
    count = metas[0].shape[1]

    @pl.when(pl.program_id(0) == 0)
    def _():
        for s in range(sources):
            meta = metas[s][...]
            routes, places = positions(meta)
            total = jnp.zeros((rows, count), F32)
            wanted = lax.broadcasted_iota(I32, (rows, count), 0)
            for k in range(TOP):
                r = routes[k]
                row = where(scalars, s, r >> 6, (r >> 2) & 15, (r >> 1) & 1, places[k])
                row = jnp.where((r & 1) == expert, row, -1)
                total = total + jnp.where(wanted == row, meta[TOP + k : TOP + k + 1, :], 0.0)
            picker[:, s * count : (s + 1) * count] = total.astype(BF)

    step = 320
    for at in range(0, rows, step):
        total = dot(picker[at : at + step, :count], tokens[0][...])
        for s in range(1, sources):
            total = total + dot(
                picker[at : at + step, s * count : (s + 1) * count], tokens[s][...]
            )
        out[at : at + step, :] = total.astype(BF)


def where_plane_first(scalars, s, dzl, dyx, dcore, place):
    core = scalars[2]
    source = core if s == 0 else 1 - core
    return jnp.where(dcore == core, dyx * 40 + dzl * 20 + source * CAP + place, -1)


def where_line_first(scalars, s, dzl, dyx, dcore, place):
    source = (scalars[0] + 4 - s) & 3
    return jnp.where(dzl == scalars[1], (dyx * 2 + dcore) * 40 + source * CAP + place, -1)


def pick(scalars, metas, tokens, rows, expert, where, block, first, blocks):
    sources = len(metas)
    count = metas[0].shape[1]
    whole = pl.BlockSpec((8, count), lambda j, s: (0, 0))
    return pl.pallas_call(
        functools.partial(pick_kernel, sources, expert, where),
        out_shape=jax.ShapeDtypeStruct((rows, blocks * block), BF),
        grid_spec=pltpu.PrefetchScalarGridSpec(
            num_scalar_prefetch=1,
            grid=(blocks,),
            in_specs=[whole] * sources
            + [
                pl.BlockSpec((count, block), functools.partial(lambda o, j, s: (0, j + o), o))
                for _, o in tokens
            ],
            out_specs=pl.BlockSpec((rows, block), lambda j, s: (0, j)),
            scratch_shapes=[pltpu.VMEM((rows, sources * count), BF)],
        ),
        compiler_params=pltpu.CompilerParams(**PARAMS),
        cost_estimate=cost(
            2 * rows * sources * count * blocks * block,
            2 * (rows + sources * count) * blocks * block,
        ),
    )(scalars, *metas, *[t for t, _ in tokens])


def part_kernel(scalars, got, own, away, picker):
    @pl.when(pl.program_id(0) == 0)
    def _():
        zl = scalars[1]
        for side, layer in ((0, zl), (1, 1 - zl)):
            row = lax.broadcasted_iota(I32, (320, 640), 0)
            source = lax.broadcasted_iota(I32, (320, 640), 1)
            group = row // 20
            hit = source == row + (group + layer) * 20
            picker[side * 320 : side * 320 + 320, :] = hit.astype(F32).astype(BF)

    away[...] = dot(picker[320:, :], got[...]).astype(BF)
    own[...] = dot(picker[:320, :], got[...]).astype(BF)


def part(scalars, got, block, first, blocks):
    shape = jax.ShapeDtypeStruct((320, blocks * block), BF)
    spec = pl.BlockSpec((320, block), lambda j, s: (0, j))
    return pl.pallas_call(
        part_kernel,
        out_shape=(shape, shape),
        grid_spec=pltpu.PrefetchScalarGridSpec(
            num_scalar_prefetch=1,
            grid=(blocks,),
            in_specs=[pl.BlockSpec((640, block), lambda j, s: (0, j + first))],
            out_specs=(spec, spec),
            scratch_shapes=[pltpu.VMEM((640, 640), BF)],
        ),
        compiler_params=pltpu.CompilerParams(**PARAMS),
        cost_estimate=cost(2 * 640 * 640 * blocks * block, 4 * 640 * blocks * block),
    )(scalars, got)


def back_kernel(pieces, has_before, *refs):
    rows, weight = refs[:pieces], refs[pieces]
    refs = refs[pieces + 1 :]
    before = refs[0] if has_before else None
    refs = refs[has_before:]
    size = rows[0].shape[0]
    if has_before:
        saved, hidden, terms, total = refs
    else:
        total = refs[0]

    @pl.when(pl.program_id(0) == 0)
    def _():
        total[...] = before[...] if has_before else jnp.zeros_like(total)

    step = 320
    for p in range(pieces):
        for at in range(0, size, step):
            total[p * size + at : p * size + at + step, :] += lax.dot_general(
                rows[p][at : at + step, :],
                weight[...],
                (((1,), (1,)), ((), ())),
                preferred_element_type=F32,
            )

    if has_before:

        @pl.when(pl.program_id(0) == pl.num_programs(0) - 1)
        def _():
            for at in range(0, pieces * size, step):
                back = total[at : at + step, :]
                hidden[at : at + step, :] = back.astype(BF)
                terms[at : at + step, :] = jnp.sum(
                    saved[at : at + step, :].astype(F32) * back, axis=1, keepdims=True
                )


def back(rows, weight, expert, block, first, blocks, before=None, saved=None):
    pieces, size = len(rows), rows[0].shape[0]
    hidden = weight.shape[1]
    shape = (pieces * size, hidden)
    whole = pl.BlockSpec(shape, lambda j: (0, 0))
    has_before = before is not None
    in_specs = [pl.BlockSpec((size, block), lambda j: (0, j))] * pieces + [
        pl.BlockSpec((None, hidden, block), lambda j: (expert, 0, j + first))
    ]
    args = [*rows, weight]
    if has_before:
        in_specs += [whole, whole]
        args += [before, saved]
        out_shape = (
            jax.ShapeDtypeStruct(shape, BF),
            jax.ShapeDtypeStruct((pieces * size, 1), F32),
        )
        out_specs = (whole, pl.BlockSpec((pieces * size, 1), lambda j: (0, 0)))
        scratch = [pltpu.VMEM(shape, F32)]
    else:
        out_shape, out_specs, scratch = jax.ShapeDtypeStruct(shape, F32), whole, []
    return pl.pallas_call(
        functools.partial(back_kernel, pieces, has_before),
        out_shape=out_shape,
        grid=(blocks,),
        in_specs=in_specs,
        out_specs=out_specs,
        scratch_shapes=scratch,
        compiler_params=pltpu.CompilerParams(**PARAMS),
        cost_estimate=cost(
            2 * pieces * size * hidden * blocks * block, 2 * pieces * size * blocks * block
        ),
    )(*args)


def down_kernel(pieces, *refs):
    saved_t, rows, out = refs[0], refs[1 : 1 + pieces], refs[-1]
    total = dot(saved_t[0], rows[0][...])
    for p in range(1, pieces):
        total = total + dot(saved_t[p], rows[p][...])
    out[...] = total.astype(BF)


def down(result, saved_t, rows, expert, block, first, blocks):
    pieces, size = len(rows), rows[0].shape[0]
    hidden = saved_t.shape[1]
    in_specs = [pl.BlockSpec(saved_t.shape, lambda j: (0, 0, 0))] + [
        pl.BlockSpec((size, block), lambda j: (0, j))
    ] * pieces
    args = [saved_t, *rows]
    width = 7 * block
    aliases = {}
    if result is not None:
        in_specs.append(pl.BlockSpec(memory_space=pl.ANY))
        args.append(result)
        aliases = {len(args) - 1: 0}
    return pl.pallas_call(
        functools.partial(down_kernel, pieces),
        out_shape=jax.ShapeDtypeStruct((2, hidden, width), BF),
        grid=(blocks,),
        in_specs=in_specs,
        out_specs=pl.BlockSpec((None, hidden, block), lambda j: (expert, 0, j + first)),
        input_output_aliases=aliases,
        compiler_params=pltpu.CompilerParams(**PARAMS),
        cost_estimate=cost(
            2 * pieces * size * hidden * blocks * block, 2 * pieces * size * blocks * block
        ),
    )(*args)


def shards(grad_out, gates, routes, w_down, saved_hidden):
    tokens, width = grad_out.shape
    zh, zl = lax.axis_index("zh"), lax.axis_index("zl")
    core = lax.axis_index("core")
    z = zh * 2 + zl
    scalars = jnp.stack([z, zl, core]).astype(I32)
    block = width // 7
    parts = ((0, 4), (4, 3))
    cut = 4 * block

    meta = jnp.concatenate([routes.T.astype(F32), gates.T.astype(F32)], axis=0)
    meta_other, other = core_swap(meta), core_swap(grad_out)
    from_down, from_up = z_shift(grad_out, 1), z_shift(grad_out, -1)
    metas = [meta, z_shift(meta, 1), z_shift(meta, 2), z_shift(meta, -1)]

    send1 = pick(
        scalars, [meta, meta_other], [(grad_out, 0), (other, 0)], 640, 1, where_plane_first,
        block, 0, 7,
    )
    got1 = lax.all_to_all(send1.reshape(16, 40, width), ("y", "x"), 0, 0, tiled=True)
    got1 = got1.reshape(640, width)

    far = (z_shift(from_down[:, :cut], 1), z_shift(from_up[:, cut:], -1))
    rows0 = []
    for (first, blocks), distant in zip(parts, far):
        send0 = pick(
            scalars, metas,
            [(grad_out, first), (from_down, first), (distant, 0), (from_up, first)],
            1280, 0, where_line_first, block, first, blocks,
        )
        got0 = lax.all_to_all(send0.reshape(32, 40, blocks * block), PLANE, 0, 0, tiled=True)
        rows0.append([got0.reshape(1280, blocks * block)])

    rows1 = []
    for first, blocks in parts:
        own, away = part(scalars, got1, block, first, blocks)
        rows1.append([own, z_shift(away, 1), z_shift(own, 2), z_shift(away, -1)])

    def swapped(a, one, two):
        return a.reshape(one, two, CAP, -1).transpose(1, 0, 2, 3).reshape(one * two * CAP, -1)

    def turned(a):
        a = a.reshape(4, 320, -1)
        return jnp.concatenate(
            [lax.dynamic_index_in_dim(a, (z - k) % 4, 0, False) for k in range(4)], axis=0
        )

    saved0 = swapped(saved_hidden[0], 4, 32)
    saved1 = turned(saved_hidden[1])
    saved0_t = saved0.T[None]
    saved1_t = saved1.reshape(4, 320, -1).transpose(0, 2, 1)

    d_down = down(None, saved1_t, rows1[0], 1, block, *parts[0])
    before1 = back(rows1[0], w_down, 1, block, *parts[0])
    d_down = down(d_down, saved0_t, rows0[0], 0, block, *parts[0])
    before0 = back(rows0[0], w_down, 0, block, *parts[0])
    d_down = down(d_down, saved1_t, rows1[1], 1, block, *parts[1])
    hidden1, terms1 = back(rows1[1], w_down, 1, block, *parts[1], before1, saved1)
    hidden0, terms0 = back(rows0[1], w_down, 0, block, *parts[1], before0, saved0)
    d_down = down(d_down, saved0_t, rows0[1], 0, block, *parts[1])
    d_hidden = jnp.stack([swapped(hidden0, 32, 4), turned(hidden1)])

    terms = jnp.concatenate(
        [swapped(terms0, 32, 4).reshape(128, CAP), turned(terms1).reshape(128, CAP)], axis=1
    )
    returned = lax.all_to_all(terms, ALL, 0, 0, tiled=True)
    returned = (returned[:64] + returned[64:]).reshape(-1)

    names = jnp.arange(EXPERTS, dtype=I32)
    onehot = routes[:, :, None] == names[None, None, :]
    order = jnp.arange(tokens, dtype=I32)
    earlier = dot(
        (order[:, None] > order[None, :]).astype(BF), jnp.any(onehot, axis=1).astype(BF)
    )
    place = jnp.sum(jnp.where(onehot, earlier[:, None, :], 0.0), axis=2).astype(I32)
    table = (routes * CAP + place).T.reshape(1, -1)
    d_gates = jnp.sum(
        jnp.where(
            table == jnp.arange(EXPERTS * CAP, dtype=I32)[:, None], returned[:, None], 0.0
        ),
        axis=0,
    ).reshape(TOP, tokens).T
    return d_gates / gates.astype(F32), d_down, d_hidden


def solution(mesh):
    fine = Mesh(mesh.devices.reshape(2, 2, 4, 4, 2), ALL)
    in_specs = (
        P(ALL, None),
        P(ALL, None),
        P(ALL, None),
        P(("zl", "y", "x", "core"), "zh", None),
        P(("zl", "y", "x", "core"), None, "zh"),
    )
    out_specs = (P(ALL, None), in_specs[3], in_specs[4])
    return jax.shard_map(shards, mesh=fine, in_specs=in_specs, out_specs=out_specs, check_vma=False)
```

```python
import functools

import jax
import jax.numpy as jnp
from jax import lax
from jax.experimental import pallas as pl
from jax.experimental.pallas import tpu as pltpu
from jax.sharding import Mesh, PartitionSpec as P

Z = ("zh", "zl")
PLANE = ("y", "x", "core")
ALL = ("zh", "zl", "y", "x", "core")
CAP = 10
TOP = 4
EXPERTS = 128
BF = jnp.bfloat16
F32 = jnp.float32
I32 = jnp.int32


def z_shift(value, step):
    return lax.ppermute(value, Z, [(i, (i + step) % 4) for i in range(4)])


def core_swap(value):
    return lax.ppermute(value, "core", [(0, 1), (1, 0)])


def dot(a, b):
    return jnp.dot(a, b, preferred_element_type=F32)


def call(body, token, args, in_specs, out_shape, out_specs, grid, micros, scratch=(), aliases=None,
         scalars=None, after=()):
    lead = 0 if scalars is None else 1
    extra = [token, *after]
    n_in, n_out = lead + len(args), len(out_shape)

    def run(*refs):
        outs = refs[n_in + len(extra) :]
        outs[n_out][...] = jnp.zeros((8, 128), F32)
        body(*refs[:n_in], *outs[:n_out], *outs[n_out + 1 :])

    result = pl.pallas_call(
        run,
        out_shape=[*out_shape, jax.ShapeDtypeStruct((8, 128), F32)],
        grid_spec=pltpu.PrefetchScalarGridSpec(
            num_scalar_prefetch=lead,
            grid=grid,
            in_specs=[*in_specs, *[pl.BlockSpec(memory_space=pl.ANY)] * len(extra)],
            out_specs=[*out_specs, pl.BlockSpec((8, 128), lambda j, *_: (0, 0))],
            scratch_shapes=list(scratch),
        ),
        input_output_aliases=aliases or {},
        compiler_params=pltpu.CompilerParams(vmem_limit_bytes=60 * 1024 * 1024),
        cost_estimate=pl.CostEstimate(
            flops=int(micros * 1e9), bytes_accessed=0, transcendentals=0
        ),
    )(*([] if scalars is None else [scalars]), *args, *extra)
    return result[:-1], result[-1]


def positions(meta):
    tokens = meta.shape[1]
    names = lax.broadcasted_iota(I32, (EXPERTS, tokens), 0)
    routes = [meta[k : k + 1, :].astype(I32) for k in range(TOP)]
    hits = [names == r for r in routes]
    named = sum(h.astype(F32) for h in hits)
    first = lax.broadcasted_iota(I32, (tokens, tokens), 0)
    second = lax.broadcasted_iota(I32, (tokens, tokens), 1)
    earlier = dot(named.astype(BF), (first < second).astype(F32).astype(BF))
    places = [
        jnp.sum(jnp.where(h, earlier, 0.0), axis=0, keepdims=True).astype(I32) for h in hits
    ]
    return routes, places


def extend_kernel(meta, tokens, out):
    count = tokens.shape[0]
    out[:count, :] = tokens[...]
    out[count:, :] = jnp.zeros((out.shape[0] - count, out.shape[1]), BF)
    out[count:, : meta.shape[1]] = jnp.concatenate(
        [meta[...], jnp.zeros_like(meta[...])], axis=0
    ).astype(BF)


def extend(token, meta, tokens):
    shape = (tokens.shape[0] + 16, tokens.shape[1])
    (out,), token = call(
        extend_kernel, token, [meta, tokens],
        [pl.BlockSpec(x.shape, lambda j: (0, 0)) for x in (meta, tokens)],
        [jax.ShapeDtypeStruct(shape, BF)], [pl.BlockSpec(shape, lambda j: (0, 0))], (1,), 0.1,
    )
    return out, token


def onward_kernel(below, *refs):
    above, down, up = refs[:3], refs[3], refs[4]
    down[...] = below[...]
    width = above[0].shape[1]
    for j in range(3):
        up[:, j * width : (j + 1) * width] = above[j][...]


def onward(token, from_down, from_up, block):
    rows = from_down.shape[0]
    shapes = [(rows, 4 * block), (rows, 3 * block)]
    return call(
        onward_kernel, token, [from_down] + [from_up] * 3,
        [pl.BlockSpec(shapes[0], lambda j: (0, 0))]
        + [
            pl.BlockSpec((rows, block), functools.partial(lambda n, j: (0, n), 4 + n))
            for n in range(3)
        ],
        [jax.ShapeDtypeStruct(sh, BF) for sh in shapes],
        [pl.BlockSpec(sh, lambda j: (0, 0)) for sh in shapes], (1,), 0.1,
    )


def prepare_kernel(scalars, saved, saved0, saved0_t, saved1, saved1_t):
    row = lax.broadcasted_iota(I32, (320, 1), 0)
    source = lax.broadcasted_iota(I32, (320, 1280), 1)
    for q in range(4):
        at = row + q * 320
        plane, line = at // 40, at % 40
        wanted = (line // CAP) * 320 + plane * CAP + line % CAP
        hit = (source == wanted).astype(F32).astype(BF)
        rows = dot(hit, saved[0])
        saved0[q * 320 : q * 320 + 320, :] = rows.astype(BF)
    saved0_t[0] = saved0[...].astype(F32).T.astype(BF)
    for k in range(4):
        at = pl.multiple_of(((scalars[0] + 4 - k) & 3) * 320, 320)
        rows = saved[1, pl.ds(at, 320), :]
        saved1[k * 320 : k * 320 + 320, :] = rows
        saved1_t[k] = rows.astype(F32).T.astype(BF)


def prepare(token, scalars, saved):
    _, rows, hidden = saved.shape
    shapes = [(rows, hidden), (1, hidden, rows), (rows, hidden), (4, hidden, rows // 4)]
    return call(
        prepare_kernel, token, [saved], [pl.BlockSpec(saved.shape, lambda j, s: (0, 0, 0))],
        [jax.ShapeDtypeStruct(sh, BF) for sh in shapes],
        [pl.BlockSpec(sh, functools.partial(lambda n, j, s: (0,) * n, len(sh))) for sh in shapes],
        (1,), 0.1, scalars=scalars,
    )


def picker_kernel(expert, where, sources, scalars, *refs):
    metas, outs = refs[:sources], refs[sources:]
    out, table = outs[0], outs[1] if len(outs) > 1 else None
    rows, count = out.shape[0], metas[0].shape[1]
    for s, ref in enumerate(metas):
        meta = ref[...].astype(F32)
        routes, places = positions(meta)
        total = jnp.zeros((rows, count), F32)
        wanted = lax.broadcasted_iota(I32, (rows, count), 0)
        for k in range(TOP):
            r = routes[k]
            row = where(scalars, s, r >> 6, (r >> 2) & 15, (r >> 1) & 1, places[k])
            row = jnp.where((r & 1) == expert, row, -1)
            total = total + jnp.where(wanted == row, meta[TOP + k : TOP + k + 1, :], 0.0)
            if table is not None and s == 0:
                table[k : k + 1, :] = r * CAP + places[k]
        out[:, s * count : (s + 1) * count] = total.astype(BF)


def picker(token, scalars, metas, specs, count, rows, expert, where, micros, table=False):
    shapes = [((rows, len(metas) * count), BF)] + [((TOP, count), I32)] * table
    return call(
        functools.partial(picker_kernel, expert, where, len(metas)),
        token, metas, specs,
        [jax.ShapeDtypeStruct(*sh) for sh in shapes],
        [pl.BlockSpec(sh[0], lambda j, s: (0, 0)) for sh in shapes],
        (1,), micros, scalars=scalars,
    )


def pick_kernel(sources, count, *refs):
    matrix, tokens, out = refs[0], refs[1 : 1 + sources], refs[-1]
    rows = matrix.shape[0]
    step = 320
    for at in range(0, rows, step):
        total = dot(matrix[at : at + step, :count], tokens[0][...])
        for s in range(1, sources):
            total = total + dot(
                matrix[at : at + step, s * count : (s + 1) * count], tokens[s][...]
            )
        out[at : at + step, :] = total.astype(BF)


def where_plane_first(scalars, s, dzl, dyx, dcore, place):
    core = scalars[2]
    source = core if s == 0 else 1 - core
    return jnp.where(dcore == core, dyx * 40 + dzl * 20 + source * CAP + place, -1)


def where_line_first(scalars, s, dzl, dyx, dcore, place):
    source = (scalars[0] + 4 - s) & 3
    return jnp.where(dzl == scalars[1], (dyx * 2 + dcore) * 40 + source * CAP + place, -1)


def pick(token, matrix, tokens, block, blocks, micros, after=()):
    rows, sources = matrix.shape[0], len(tokens)
    count = matrix.shape[1] // sources
    (out,), token = call(
        functools.partial(pick_kernel, sources, count),
        token, [matrix, *[t for t, _ in tokens]],
        [pl.BlockSpec(matrix.shape, lambda j: (0, 0))]
        + [
            pl.BlockSpec((count, block), functools.partial(lambda o, j: (0, j + o), o))
            for _, o in tokens
        ],
        [jax.ShapeDtypeStruct((rows, blocks * block), BF)],
        [pl.BlockSpec((rows, block), lambda j: (0, j))],
        (blocks,), micros, after=after,
    )
    return out, token


def part_kernel(scalars, got, own, away, picker):
    @pl.when(pl.program_id(0) == 0)
    def _():
        zl = scalars[1]
        for side, layer in ((0, zl), (1, 1 - zl)):
            row = lax.broadcasted_iota(I32, (320, 640), 0)
            source = lax.broadcasted_iota(I32, (320, 640), 1)
            group = row // 20
            hit = source == row + (group + layer) * 20
            picker[side * 320 : side * 320 + 320, :] = hit.astype(F32).astype(BF)

    away[...] = dot(picker[320:, :], got[...]).astype(BF)
    own[...] = dot(picker[:320, :], got[...]).astype(BF)


def part(token, scalars, got, block, first, blocks):
    shape = jax.ShapeDtypeStruct((320, blocks * block), BF)
    spec = pl.BlockSpec((320, block), lambda j, s: (0, j))
    return call(
        part_kernel, token, [got], [pl.BlockSpec((640, block), lambda j, s: (0, j + first))],
        [shape, shape], [spec, spec], (blocks,), 0.1, scratch=[pltpu.VMEM((640, 640), BF)],
        scalars=scalars,
    )


def back_kernel(pieces, has_before, *refs):
    rows, weight = refs[:pieces], refs[pieces]
    refs = refs[pieces + 1 :]
    before = refs[0] if has_before else None
    refs = refs[has_before:]
    size = rows[0].shape[0]
    if has_before:
        saved, hidden, terms, total = refs
    else:
        total = refs[0]

    @pl.when(pl.program_id(0) == 0)
    def _():
        total[...] = before[...] if has_before else jnp.zeros_like(total)

    step = 320
    for p in range(pieces):
        for at in range(0, size, step):
            total[p * size + at : p * size + at + step, :] += lax.dot_general(
                rows[p][at : at + step, :],
                weight[...],
                (((1,), (1,)), ((), ())),
                preferred_element_type=F32,
            )

    if has_before:

        @pl.when(pl.program_id(0) == pl.num_programs(0) - 1)
        def _():
            for at in range(0, pieces * size, step):
                back = total[at : at + step, :]
                hidden[at : at + step, :] = back.astype(BF)
                terms[at : at + step, :] = jnp.sum(
                    saved[at : at + step, :].astype(F32) * back, axis=1, keepdims=True
                )


def back(
    token, rows, weight, expert, block, first, blocks, before=None, saved=None, micros=0.1
):
    pieces, size = len(rows), rows[0].shape[0]
    hidden = weight.shape[1]
    shape = (pieces * size, hidden)
    whole = pl.BlockSpec(shape, lambda j: (0, 0))
    has_before = before is not None
    in_specs = [pl.BlockSpec((size, block), lambda j: (0, j))] * pieces + [
        pl.BlockSpec((None, hidden, block), lambda j: (expert, 0, j + first))
    ]
    args = [*rows, weight]
    if has_before:
        in_specs += [whole, whole]
        args += [before, saved]
        out_shape = [
            jax.ShapeDtypeStruct(shape, BF),
            jax.ShapeDtypeStruct((pieces * size, 1), F32),
        ]
        out_specs = [whole, pl.BlockSpec((pieces * size, 1), lambda j: (0, 0))]
        scratch = [pltpu.VMEM(shape, F32)]
    else:
        out_shape, out_specs, scratch = [jax.ShapeDtypeStruct(shape, F32)], [whole], []
    return call(
        functools.partial(back_kernel, pieces, has_before),
        token, args, in_specs, out_shape, out_specs, (blocks,), micros, scratch=scratch,
    )


def down_kernel(pieces, *refs):
    saved_t, rows, out = refs[0], refs[1 : 1 + pieces], refs[-1]
    total = dot(saved_t[0], rows[0][...])
    for p in range(1, pieces):
        total = total + dot(saved_t[p], rows[p][...])
    out[...] = total.astype(BF)


def down(token, result, saved_t, rows, expert, block, first, blocks):
    pieces, size = len(rows), rows[0].shape[0]
    hidden = saved_t.shape[1]
    in_specs = [pl.BlockSpec(saved_t.shape, lambda j: (0, 0, 0))] + [
        pl.BlockSpec((size, block), lambda j: (0, j))
    ] * pieces
    args = [saved_t, *rows]
    aliases = {}
    if result is not None:
        in_specs.append(pl.BlockSpec(memory_space=pl.ANY))
        args.append(result)
        aliases = {len(args) - 1: 0}
    (out,), token = call(
        functools.partial(down_kernel, pieces),
        token, args, in_specs,
        [jax.ShapeDtypeStruct((2, hidden, 7 * block), BF)],
        [pl.BlockSpec((None, hidden, block), lambda j: (expert, 0, j + first))],
        (blocks,), 0.1, aliases=aliases,
    )
    return out, token


def finish_kernel(scalars, hidden0, hidden1, out):
    for k in range(4):
        at = pl.multiple_of(((scalars[0] + 4 - k) & 3) * 320, 320)
        out[1, pl.ds(at, 320), :] = hidden1[k * 320 : k * 320 + 320, :]
    row = lax.broadcasted_iota(I32, (320, 1), 0)
    wanted = row + (row // CAP) * (3 * CAP)
    source = lax.broadcasted_iota(I32, (320, 1280), 1)
    for k in range(4):
        hit = (source == wanted + k * CAP).astype(F32).astype(BF)
        out[0, k * 320 : k * 320 + 320, :] = dot(hit, hidden0[...]).astype(BF)


def finish(token, scalars, hidden0, hidden1):
    shape = (2, *hidden0.shape)
    whole = pl.BlockSpec(hidden0.shape, lambda j, s: (0, 0))
    (out,), token = call(
        finish_kernel, token, [hidden0, hidden1], [whole, whole],
        [jax.ShapeDtypeStruct(shape, BF)], [pl.BlockSpec(shape, lambda j, s: (0, 0, 0))],
        (1,), 0.1, scalars=scalars,
    )
    return out


def shards(grad_out, gates, routes, w_down, saved_hidden):
    tokens, width = grad_out.shape
    zh, zl = lax.axis_index("zh"), lax.axis_index("zl")
    core = lax.axis_index("core")
    z = zh * 2 + zl
    scalars = jnp.stack([z, zl, core]).astype(I32)
    block = width // 7
    parts = ((0, 4), (4, 3))

    meta = jnp.concatenate([routes.T.astype(F32), gates.T.astype(F32)], axis=0)
    meta_other, other = core_swap(meta), core_swap(grad_out)
    token = jnp.zeros((8, 128), F32)
    extended, token = extend(token, meta, grad_out)
    from_down, from_up = z_shift(extended, 1), z_shift(extended, -1)
    meta_far = z_shift(meta, 2)
    (matrix1, table), token = picker(
        token, scalars, [meta, meta_other],
        [pl.BlockSpec(meta.shape, lambda j, s: (0, 0))] * 2,
        tokens, 640, 1, where_plane_first, 0.1, True,
    )
    send1, token = pick(token, matrix1, [(grad_out, 0), (other, 0)], block, 7, 0.1)
    got1 = lax.all_to_all(send1.reshape(16, 40, width), ("y", "x"), 0, 0, tiled=True)
    got1 = got1.reshape(640, width)

    (saved0, saved0_t, saved1, saved1_t), token = prepare(token, scalars, saved_hidden)
    (onward_down, onward_up), token = onward(token, from_down, from_up, block)
    far = (z_shift(onward_down, 1), z_shift(onward_up, -1))
    below = pl.BlockSpec((16, tokens), lambda j, s: (tokens // 16, 0))
    (matrix0,), token = picker(
        token, scalars, [extended, from_down, meta_far, from_up],
        [below, below, pl.BlockSpec(meta.shape, lambda j, s: (0, 0)), below],
        tokens, 1280, 0, where_line_first, 200,
    )

    def line(c):
        first, blocks = parts[c]
        return [(extended, first), (from_down, first), (far[c], 0), (from_up, first)]

    def exchange0(send):
        got = lax.all_to_all(send.reshape(32, 40, -1), PLANE, 0, 0, tiled=True)
        return [got.reshape(1280, -1)]

    send0, token = pick(token, matrix0, line(0), block, parts[0][1], 200, after=[far[1]])
    rows0 = [exchange0(send0)]
    rows1 = []
    for first, blocks in parts:
        (own, away), token = part(token, scalars, got1, block, first, blocks)
        rows1.append([own, z_shift(away, 1), z_shift(own, 2), z_shift(away, -1)])
    send0, token = pick(token, matrix0, line(1), block, parts[1][1], 0.1)
    rows0.append(exchange0(send0))

    (before0,), token = back(token, rows0[0], w_down, 0, block, *parts[0])
    d_down, token = down(token, None, saved0_t, rows0[0], 0, block, *parts[0])
    (before1,), token = back(token, rows1[0], w_down, 1, block, *parts[0])
    d_down, token = down(token, d_down, saved1_t, rows1[0], 1, block, *parts[0])
    (hidden1, terms1), token = back(
        token, rows1[1], w_down, 1, block, *parts[1], before1, saved1, 200
    )
    (hidden0, terms0), token = back(
        token, rows0[1], w_down, 0, block, *parts[1], before0, saved0
    )
    d_down, token = down(token, d_down, saved1_t, rows1[1], 1, block, *parts[1])
    d_down, token = down(token, d_down, saved0_t, rows0[1], 0, block, *parts[1])
    d_hidden = finish(token, scalars, hidden0, hidden1)

    def swapped(a, one, two):
        return a.reshape(one, two, CAP, -1).transpose(1, 0, 2, 3).reshape(one * two * CAP, -1)

    def turned(a):
        a = a.reshape(4, 320, -1)
        return jnp.concatenate(
            [lax.dynamic_index_in_dim(a, (z - k) % 4, 0, False) for k in range(4)], axis=0
        )

    terms = jnp.concatenate(
        [swapped(terms0, 32, 4).reshape(128, CAP), turned(terms1).reshape(128, CAP)], axis=1
    )
    returned = lax.all_to_all(terms, ALL, 0, 0, tiled=True)
    returned = (returned[:64] + returned[64:]).reshape(-1)

    table = table.reshape(1, -1)
    d_gates = jnp.sum(
        jnp.where(
            table == jnp.arange(EXPERTS * CAP, dtype=I32)[:, None], returned[:, None], 0.0
        ),
        axis=0,
    ).reshape(TOP, tokens).T
    return d_gates / gates.astype(F32), d_down, d_hidden


def solution(mesh):
    fine = Mesh(mesh.devices.reshape(2, 2, 4, 4, 2), ALL)
    in_specs = (
        P(ALL, None),
        P(ALL, None),
        P(ALL, None),
        P(("zl", "y", "x", "core"), "zh", None),
        P(("zl", "y", "x", "core"), None, "zh"),
    )
    out_specs = (P(ALL, None), in_specs[3], in_specs[4])
    return jax.shard_map(shards, mesh=fine, in_specs=in_specs, out_specs=out_specs, check_vma=False)
```

```python
import functools

import jax
import jax.numpy as jnp
from jax import lax
from jax.experimental import pallas as pl
from jax.experimental.pallas import tpu as pltpu
from jax.sharding import Mesh, PartitionSpec as P

Z = ("zh", "zl")
PLANE = ("y", "x", "core")
ALL = ("zh", "zl", "y", "x", "core")
CAP = 10
TOP = 4
STEPS = (0, 1, 3, 2)
EXPERTS = 128
BF = jnp.bfloat16
F32 = jnp.float32
I32 = jnp.int32


def z_shift(value, step):
    return lax.ppermute(value, Z, [(i, (i + step) % 4) for i in range(4)])


def core_swap(value):
    return lax.ppermute(value, "core", [(0, 1), (1, 0)])


def dot(a, b):
    return jnp.dot(a, b, preferred_element_type=F32)


def call(body, token, args, in_specs, out_shape, out_specs, grid, micros, scratch=(), aliases=None,
         scalars=None, after=()):
    lead = 0 if scalars is None else 1
    extra = [*([] if token is None else [token]), *after]
    n_in, n_out = lead + len(args), len(out_shape)

    def run(*refs):
        outs = refs[n_in + len(extra) :]
        outs[n_out][...] = jnp.zeros((8, 128), F32)
        body(*refs[:n_in], *outs[:n_out], *outs[n_out + 1 :])

    result = pl.pallas_call(
        run,
        out_shape=[*out_shape, jax.ShapeDtypeStruct((8, 128), F32)],
        grid_spec=pltpu.PrefetchScalarGridSpec(
            num_scalar_prefetch=lead,
            grid=grid,
            in_specs=[*in_specs, *[pl.BlockSpec(memory_space=pl.ANY)] * len(extra)],
            out_specs=[*out_specs, pl.BlockSpec((8, 128), lambda j, *_: (0, 0))],
            scratch_shapes=list(scratch),
        ),
        input_output_aliases=aliases or {},
        compiler_params=pltpu.CompilerParams(vmem_limit_bytes=60 * 1024 * 1024),
        cost_estimate=pl.CostEstimate(
            flops=int(micros * 1e9), bytes_accessed=0, transcendentals=0
        ),
    )(*([] if scalars is None else [scalars]), *args, *extra)
    return result[:-1], result[-1]


def positions(meta):
    tokens = meta.shape[1]
    names = lax.broadcasted_iota(I32, (EXPERTS, tokens), 0)
    routes = [meta[k : k + 1, :].astype(I32) for k in range(TOP)]
    hits = [names == r for r in routes]
    named = sum(h.astype(F32) for h in hits)
    first = lax.broadcasted_iota(I32, (tokens, tokens), 0)
    second = lax.broadcasted_iota(I32, (tokens, tokens), 1)
    earlier = dot(named.astype(BF), (first < second).astype(F32).astype(BF))
    places = [
        jnp.sum(jnp.where(h, earlier, 0.0), axis=0, keepdims=True).astype(I32) for h in hits
    ]
    return routes, places


def onward_kernel(below, above, meta, down, up, meta_out):
    cut = down.shape[1]
    down[...] = below[:, :cut]
    up[...] = above[:, cut:]
    meta_out[...] = meta[...]


def onward(token, from_down, from_up, meta, cut):
    rows, width = from_down.shape
    shapes = [((rows, cut), BF), ((rows, width - cut), BF), (meta.shape, F32)]
    return call(
        onward_kernel, token, [from_down, from_up, meta],
        [
            pl.BlockSpec((rows, cut), lambda j: (0, 0)),
            pl.BlockSpec((rows, width), lambda j: (0, 0)),
            pl.BlockSpec(meta.shape, lambda j: (0, 0)),
        ],
        [jax.ShapeDtypeStruct(*sh) for sh in shapes],
        [pl.BlockSpec(sh[0], lambda j: (0, 0)) for sh in shapes], (1,), 1000,
    )


def prepare_kernel(scalars, saved, saved0, saved0_t, near, near_t, distant, distant_t):
    row = lax.broadcasted_iota(I32, (320, 1), 0)
    source = lax.broadcasted_iota(I32, (320, 1280), 1)
    for q in range(4):
        at = row + q * 320
        plane, line = at // 40, at % 40
        z = jnp.where(line < 32, line // 8, (line - 32) // 2)
        place = jnp.where(line < 32, line % 8, 8 + line % 2)
        hit = (source == z * 320 + plane * CAP + place).astype(F32).astype(BF)
        rows = dot(hit, saved[0])
        saved0[q * 320 : q * 320 + 320, :] = rows.astype(BF)
    saved0_t[...] = saved0[...].astype(F32).T.astype(BF)
    for at, step in enumerate(STEPS):
        begin = pl.multiple_of(((scalars[0] + 4 - step) & 3) * 320, 320)
        rows = saved[1, pl.ds(begin, 320), :]
        if at < 3:
            near[at * 320 : at * 320 + 320, :] = rows
        else:
            distant[...] = rows
    near_t[...] = near[...].astype(F32).T.astype(BF)
    distant_t[...] = distant[...].astype(F32).T.astype(BF)


def prepare(token, scalars, saved):
    _, rows, hidden = saved.shape
    shapes = [(n, hidden)[::turn] for n in (rows, rows * 3 // 4, rows // 4) for turn in (1, -1)]
    return call(
        prepare_kernel, token, [saved], [pl.BlockSpec(saved.shape, lambda j, s: (0, 0, 0))],
        [jax.ShapeDtypeStruct(sh, BF) for sh in shapes],
        [pl.BlockSpec(sh, lambda j, s: (0, 0)) for sh in shapes],
        (1,), 0.1, scalars=scalars,
    )


def picked(meta, rows_of, rows):
    routes, places = positions(meta)
    total = jnp.zeros((rows, meta.shape[1]), F32)
    wanted = lax.broadcasted_iota(I32, total.shape, 0)
    for k in range(TOP):
        row = rows_of(routes[k], places[k])
        total = total + jnp.where(wanted == row, meta[TOP + k : TOP + k + 1, :], 0.0)
    return total.astype(BF), routes, places


def first_picker_kernel(scalars, routes, gates, routes_other, gates_other, out, table, meta):
    core = scalars[2]
    count = meta.shape[1]
    for s, pair in enumerate(((routes, gates), (routes_other, gates_other))):
        both = jnp.concatenate([x[...].astype(F32) for x in pair], axis=0)
        source = core if s == 0 else 1 - core

        def rows_of(r, place):
            row = ((r >> 2) & 15) * 40 + (r >> 6) * 20 + source * CAP + place
            return jnp.where((r & 3) == 2 * core + 1, row, -1)

        matrix, named, places = picked(both, rows_of, out.shape[0])
        out[:, s * count : (s + 1) * count] = matrix
        if s == 0:
            meta[...] = both
            for k in range(TOP):
                r = named[k]
                device = ((r >> 1) & 31) * 4 + (r >> 6) * 2
                table[k : k + 1, :] = (device + (r & 1)) * CAP + places[k]


def first_picker(scalars, *args):
    count = args[0].shape[1]
    shapes = [((640, 2 * count), BF), ((TOP, count), I32), ((2 * TOP, count), F32)]
    return call(
        first_picker_kernel, None, args, [pl.BlockSpec(x.shape, lambda j, s: (0, 0)) for x in args],
        [jax.ShapeDtypeStruct(*sh) for sh in shapes],
        [pl.BlockSpec(sh[0], lambda j, s: (0, 0)) for sh in shapes], (1,), 0.1, scalars=scalars,
    )


def line_picker_kernel(scalars, *refs):
    metas, (first, last) = refs[:4], refs[4:]
    count = metas[0].shape[1]
    for s in range(4):
        source = (scalars[0] + 4 - s) & 3

        def rows_of(r, place, low, high, at):
            mine = ((r >> 6) == scalars[1]) & ((r & 1) == 0) & (place >= low) & (place < high)
            return jnp.where(mine, ((r >> 1) & 31) * 8 + at + place - low, -1)

        meta = metas[s][...]
        routes, places = positions(meta)
        wanted = lax.broadcasted_iota(I32, (256, count), 0)
        for out, low, high, at in ((first, 0, 8, 0), (last, 8, CAP, source * 2)):
            total = jnp.zeros((256, count), F32)
            for k in range(TOP):
                row = rows_of(routes[k], places[k], low, high, at)
                total = total + jnp.where(wanted == row, meta[TOP + k : TOP + k + 1, :], 0.0)
            out[:, s * count : (s + 1) * count] = total.astype(BF)


def line_picker(token, scalars, metas):
    count = metas[0].shape[1]
    shape = (256, 4 * count)
    return call(
        line_picker_kernel, token, metas,
        [pl.BlockSpec(x.shape, lambda j, s: (0, 0)) for x in metas],
        [jax.ShapeDtypeStruct(shape, BF)] * 2, [pl.BlockSpec(shape, lambda j, s: (0, 0))] * 2,
        (1,), 0.1, scalars=scalars,
    )


def pick_kernel(matrix, one, two, out):
    lines = jnp.concatenate([one[...], two[...]], axis=0)
    out[...] = dot(matrix[...], lines).astype(BF)


def pick(token, matrix, tokens, block):
    (count, width), rows = tokens[0].shape, matrix.shape[0]
    (out,), token = call(
        pick_kernel, token, [matrix, *tokens],
        [pl.BlockSpec(matrix.shape, lambda j: (0, 0))]
        + [pl.BlockSpec((count, block), lambda j: (0, j))] * 2,
        [jax.ShapeDtypeStruct((rows, width), BF)],
        [pl.BlockSpec((rows, block), lambda j: (0, j))], (width // block,), 0.1,
    )
    return out, token


def line_pick_kernel(scalars, first, last, here, down, far_left, far_right, up, out):
    count = here.shape[0]
    left = pl.program_id(0) < pl.num_programs(0) // 2
    far = jnp.where(left, far_left[...], far_right[...])
    tokens = [here[...], down[...], far, up[...]]

    def grouped(rows):
        return rows.reshape(32, 8, rows.shape[1]).astype(BF)

    for s in range(4):
        source = (scalars[0] + 4 - s) & 3
        out[:, source] = grouped(dot(first[:, s * count : (s + 1) * count], tokens[s]))
    out[:, 4] = grouped(dot(last[...], jnp.concatenate(tokens, axis=0)))


def line_pick(token, scalars, matrices, here, down, far, up, block):
    count, width = here.shape
    half = width // block // 2
    every = pl.BlockSpec((count, block), lambda j, s: (0, j))
    (out,), token = call(
        line_pick_kernel, token, [*matrices, here, down, *far, up],
        [pl.BlockSpec(m.shape, lambda j, s: (0, 0)) for m in matrices]
        + [
            every, every,
            pl.BlockSpec((count, block), lambda j, s: (0, jnp.minimum(j, half - 1))),
            pl.BlockSpec((count, block), lambda j, s: (0, jnp.maximum(j - half, 0))),
            every,
        ],
        [jax.ShapeDtypeStruct((32, 5, 8, width), BF)],
        [pl.BlockSpec((32, 5, 8, block), lambda j, s: (0, 0, 0, j))],
        (2 * half,), 0.1, scalars=scalars,
    )
    return out, token


def part_kernel(other, scalars, got, *refs):
    out, picker = refs[-3 if other else -2], refs[-1]
    layer = 1 - scalars[1] if other else scalars[1]

    @pl.when(pl.program_id(0) == 0)
    def _():
        row = lax.broadcasted_iota(I32, (160, 1), 0)
        source = lax.broadcasted_iota(I32, (160, 320), 1)
        picker[...] = (source == row + (row // 20 + layer) * 20).astype(F32).astype(BF)

    for half in range(2):
        rows = dot(picker[...], got[half * 320 : half * 320 + 320, :])
        out[half * 160 : half * 160 + 160, :] = rows.astype(BF)


def part(token, scalars, got, carried=None, after=()):
    width = got.shape[1]
    wide = width // 2
    other = carried is not None
    anywhere = [pl.BlockSpec(memory_space=pl.ANY)] * other
    result, token = call(
        functools.partial(part_kernel, other), token, [got] + [carried] * other,
        [pl.BlockSpec((640, wide), lambda j, s: (0, j)), *anywhere],
        [jax.ShapeDtypeStruct((320, width), BF)]
        + [jax.ShapeDtypeStruct(carried.shape, BF) for _ in anywhere],
        [pl.BlockSpec((320, wide), lambda j, s: (0, j)), *anywhere],
        (2,), 0.1, scratch=[pltpu.VMEM((160, 320), BF)], scalars=scalars, after=after,
        aliases={2: 1} if other else {},
    )
    return result, token


def lines_of(rows):
    return jnp.concatenate([r[...] for r in rows], axis=0)


def back_kernel(pieces, *refs):
    rows, (weight, saved, hidden, terms, total) = refs[:pieces], refs[pieces:]

    @pl.when(pl.program_id(0) == 0)
    def _():
        total[...] = jnp.zeros_like(total)

    total[...] += lax.dot_general(
        lines_of(rows), weight[...], (((1,), (1,)), ((), ())), preferred_element_type=F32
    )

    @pl.when(pl.program_id(0) == pl.num_programs(0) - 1)
    def _():
        hidden[...] = total[...].astype(BF)
        products = saved[...].astype(F32) * total[...]
        lanes = sum(products[:, at : at + 128] for at in range(0, products.shape[1], 128))
        terms[...] = jnp.sum(lanes.T, axis=0, keepdims=True)


def back(token, rows, weight, saved, expert):
    shape = saved.shape
    block = weight.shape[2] // 2
    whole = pl.BlockSpec(shape, lambda j: (0, 0))
    return call(
        functools.partial(back_kernel, len(rows)), token, [*rows, weight, saved],
        [pl.BlockSpec((rows[0].shape[0], block), lambda j: (0, j))] * len(rows)
        + [pl.BlockSpec((None, shape[1], block), lambda j: (expert, 0, j)), whole],
        [jax.ShapeDtypeStruct(shape, BF), jax.ShapeDtypeStruct((1, shape[0]), F32)],
        [whole, pl.BlockSpec((1, shape[0]), lambda j: (0, 0))],
        (2,), 0.1, scratch=[pltpu.VMEM(shape, F32)],
    )


def down_kernel(pieces, before, saved_t, *refs):
    rows, out = refs[:pieces], refs[-1]
    total = dot(saved_t[...], lines_of(rows))
    if before:
        total = total + refs[pieces][...]
    out[...] = total.astype(out.dtype)


def down(token, saved_t, rows, width, expert=None, before=None, result=None):
    hidden = saved_t.shape[0]
    block = width // 2
    column = pl.BlockSpec((hidden, block), lambda j: (0, j))
    in_specs = [pl.BlockSpec(saved_t.shape, lambda j: (0, 0)), *[pl.BlockSpec((rows[0].shape[0], block), lambda j: (0, j))] * len(rows)]
    args = [saved_t, *rows]
    if before is not None:
        in_specs.append(column)
        args.append(before)
    aliases = {}
    if result is not None:
        in_specs.append(pl.BlockSpec(memory_space=pl.ANY))
        args.append(result)
        aliases = {len(args) - 1: 0}
    if expert is None:
        out_shape, out_spec = jax.ShapeDtypeStruct((hidden, width), F32), column
    else:
        out_shape = jax.ShapeDtypeStruct((2, hidden, width), BF)
        out_spec = pl.BlockSpec((None, hidden, block), lambda j: (expert, 0, j))
    (out,), token = call(
        functools.partial(down_kernel, len(rows), before is not None), token, args,
        in_specs, [out_shape], [out_spec], (2,), 0.1, aliases=aliases,
    )
    return out, token


def finish_kernel(scalars, hidden0, near, distant, out):
    z = pl.program_id(0)
    step = (scalars[0] + 4 - z) & 3
    begin = pl.multiple_of(jnp.where(step == 3, 2, step & 1) * 320, 320)
    out[1] = jnp.where(step == 2, distant[...], near[pl.ds(begin, 320), :])
    row = lax.broadcasted_iota(I32, (160, 1), 0)
    plane, place = row // CAP, row % CAP
    source = lax.broadcasted_iota(I32, (160, 640), 1)
    line = jnp.where(place < 8, z * 8 + place, 24 + z * 2 + place)
    hit = (source == plane * 40 + line).astype(F32).astype(BF)
    for half in range(2):
        rows = dot(hit, hidden0[half * 640 : half * 640 + 640, :])
        out[0, half * 160 : half * 160 + 160, :] = rows.astype(BF)


def finish(token, scalars, *args):
    rows, hidden = args[0].shape
    (out,), token = call(
        finish_kernel, token, args, [pl.BlockSpec(x.shape, lambda j, s: (0, 0)) for x in args],
        [jax.ShapeDtypeStruct((2, rows, hidden), BF)],
        [pl.BlockSpec((2, rows // 4, hidden), lambda j, s: (0, j, 0))],
        (4,), 0.1, scalars=scalars,
    )
    return out


def shards(grad_out, gates, routes, w_down, saved_hidden):
    tokens, width = grad_out.shape
    zh, zl = lax.axis_index("zh"), lax.axis_index("zl")
    core = lax.axis_index("core")
    z = zh * 2 + zl
    scalars = jnp.stack([z, zl, core]).astype(I32)

    wide = width // 2

    from_down, from_up = z_shift(grad_out, 1), z_shift(grad_out, -1)
    slots = (routes.T, gates.T)
    other = core_swap(grad_out)
    (matrix1, table, meta), token = first_picker(scalars, *slots, *[core_swap(x) for x in slots])
    send1, token = pick(token, matrix1, [grad_out, other], wide)
    got1 = lax.all_to_all(send1.reshape(16, 40, width), ("y", "x"), 0, 0, tiled=True)
    got1 = got1.reshape(640, width)

    (onward_down, onward_up, meta), token = onward(token, from_down, from_up, meta, wide)
    metas = [meta, z_shift(meta, 1), z_shift(meta, 2), z_shift(meta, -1)]
    far = (z_shift(onward_down, 1), z_shift(onward_up, -1))
    saved, token = prepare(token, scalars, saved_hidden)
    saved0, saved0_t, saved_near, saved_near_t, saved_distant, saved_distant_t = saved
    matrices, token = line_picker(token, scalars, metas)

    send0, token = line_pick(
        token, scalars, matrices, grad_out, from_down, far, from_up, width // 4
    )
    (away, send0), token = part(token, scalars, got1, send0)
    rows0 = lax.all_to_all(send0, PLANE, 0, 0, tiled=True).reshape(1280, width)
    near = [z_shift(away, 1), z_shift(away, -1)]
    (own,), token = part(token, scalars, got1, None, near)
    near = [own, *near]
    distant = [z_shift(own, 2)]

    (hidden_near, terms_near), token = back(token, near, w_down, saved_near, 1)
    before, token = down(token, saved_near_t, near, width)
    (hidden0, terms0), token = back(token, [rows0], w_down, saved0, 0)
    (hidden_distant, terms_distant), token = back(token, distant, w_down, saved_distant, 1)
    d_down, token = down(token, saved_distant_t, distant, width, 1, before)
    d_down, token = down(token, saved0_t, [rows0], width, 0, None, d_down)
    d_hidden = finish(token, scalars, hidden0, hidden_near, hidden_distant)

    terms_near = terms_near.reshape(3, 32, CAP)
    terms1 = jnp.stack(
        [terms_near[0], terms_near[1], terms_distant.reshape(32, CAP), terms_near[2]], axis=1
    )
    terms1 = jnp.concatenate(
        [lax.dynamic_index_in_dim(terms1, (z - i) % 4, 1, True) for i in range(4)], axis=1
    )
    terms0 = terms0.reshape(32, 40)
    terms0 = jnp.concatenate(
        [terms0[:, :32].reshape(32, 4, 8), terms0[:, 32:].reshape(32, 4, 2)], axis=2
    )
    terms = jnp.concatenate([terms0, terms1], axis=2).reshape(128, 2 * CAP)
    returned = lax.all_to_all(terms, PLANE + Z, 0, 0, tiled=True)
    returned = returned.reshape(32, 2, 2, 2 * CAP)
    returned = (returned[:, 0] + returned[:, 1]).reshape(-1)

    table = table.reshape(1, -1)
    d_gates = jnp.sum(
        jnp.where(
            table == jnp.arange(EXPERTS * CAP, dtype=I32)[:, None], returned[:, None], 0.0
        ),
        axis=0,
    ).reshape(TOP, tokens).T
    return d_gates / gates.astype(F32), d_down, d_hidden


def solution(mesh):
    fine = Mesh(mesh.devices.reshape(2, 2, 4, 4, 2), ALL)
    in_specs = (
        P(ALL, None),
        P(ALL, None),
        P(ALL, None),
        P(("zl", "y", "x", "core"), "zh", None),
        P(("zl", "y", "x", "core"), None, "zh"),
    )
    out_specs = (P(ALL, None), in_specs[3], in_specs[4])
    return jax.shard_map(shards, mesh=fine, in_specs=in_specs, out_specs=out_specs, check_vma=False)
```

```python
import functools

import jax
import jax.numpy as jnp
from jax import lax
from jax.experimental import pallas as pl
from jax.experimental.pallas import tpu as pltpu
from jax.sharding import Mesh, PartitionSpec as P

Z = ("zh", "zl")
PLANE = ("y", "x", "core")
ALL = ("zh", "zl", "y", "x", "core")
CAP = 10
TOP = 4
STEPS = (0, 1, 3, 2)
EXPERTS = 128
BF = jnp.bfloat16
F32 = jnp.float32
I32 = jnp.int32


def z_shift(value, step):
    return lax.ppermute(value, Z, [(i, (i + step) % 4) for i in range(4)])


def core_swap(value):
    return lax.ppermute(value, "core", [(0, 1), (1, 0)])


def dot(a, b):
    return jnp.dot(a, b, preferred_element_type=F32)


def call(body, token, args, in_specs, out_shape, out_specs, grid, micros, scratch=(), aliases=None,
         scalars=None, after=()):
    lead = 0 if scalars is None else 1
    extra = [*([] if token is None else [token]), *after]
    n_in, n_out = lead + len(args), len(out_shape)

    def run(*refs):
        outs = refs[n_in + len(extra) :]
        outs[n_out][...] = jnp.zeros((8, 128), F32)
        body(*refs[:n_in], *outs[:n_out], *outs[n_out + 1 :])

    result = pl.pallas_call(
        run,
        out_shape=[*out_shape, jax.ShapeDtypeStruct((8, 128), F32)],
        grid_spec=pltpu.PrefetchScalarGridSpec(
            num_scalar_prefetch=lead,
            grid=grid,
            in_specs=[*in_specs, *[pl.BlockSpec(memory_space=pl.ANY)] * len(extra)],
            out_specs=[*out_specs, pl.BlockSpec((8, 128), lambda j, *_: (0, 0))],
            scratch_shapes=list(scratch),
        ),
        input_output_aliases=aliases or {},
        compiler_params=pltpu.CompilerParams(vmem_limit_bytes=60 * 1024 * 1024),
        cost_estimate=pl.CostEstimate(
            flops=int(micros * 1e9), bytes_accessed=0, transcendentals=0
        ),
    )(*([] if scalars is None else [scalars]), *args, *extra)
    return result[:-1], result[-1]


def positions(meta):
    tokens = meta.shape[1]
    names = lax.broadcasted_iota(I32, (EXPERTS, tokens), 0)
    routes = [meta[k : k + 1, :].astype(I32) for k in range(TOP)]
    hits = [names == r for r in routes]
    named = sum(h.astype(F32) for h in hits)
    first = lax.broadcasted_iota(I32, (tokens, tokens), 0)
    second = lax.broadcasted_iota(I32, (tokens, tokens), 1)
    earlier = dot(named.astype(BF), (first < second).astype(F32).astype(BF))
    places = [
        jnp.sum(jnp.where(h, earlier, 0.0), axis=0, keepdims=True).astype(I32) for h in hits
    ]
    return routes, places


def onward_kernel(below, above, meta, down, up, meta_out):
    cut = down.shape[1]
    down[...] = below[:, :cut]
    up[...] = above[:, cut:]
    meta_out[...] = meta[...]


def onward(token, from_down, from_up, meta, cut):
    rows, width = from_down.shape
    shapes = [((rows, cut), BF), ((rows, width - cut), BF), (meta.shape, F32)]
    return call(
        onward_kernel, token, [from_down, from_up, meta],
        [
            pl.BlockSpec((rows, cut), lambda j: (0, 0)),
            pl.BlockSpec((rows, width), lambda j: (0, 0)),
            pl.BlockSpec(meta.shape, lambda j: (0, 0)),
        ],
        [jax.ShapeDtypeStruct(*sh) for sh in shapes],
        [pl.BlockSpec(sh[0], lambda j: (0, 0)) for sh in shapes], (1,), 1000,
    )


def prepare_kernel(scalars, saved, saved0, saved0_t, near, near_t, distant, distant_t):
    row = lax.broadcasted_iota(I32, (320, 1), 0)
    source = lax.broadcasted_iota(I32, (320, 1280), 1)
    for q in range(4):
        at = row + q * 320
        plane, line = at // 40, at % 40
        z = jnp.where(line < 32, line // 8, (line - 32) // 2)
        place = jnp.where(line < 32, line % 8, 8 + line % 2)
        hit = (source == z * 320 + plane * CAP + place).astype(F32).astype(BF)
        rows = dot(hit, saved[0])
        saved0[q * 320 : q * 320 + 320, :] = rows.astype(BF)
    saved0_t[...] = saved0[...].astype(F32).T.astype(BF)
    for at, step in enumerate(STEPS):
        begin = pl.multiple_of(((scalars[0] + 4 - step) & 3) * 320, 320)
        rows = saved[1, pl.ds(begin, 320), :]
        if at < 3:
            near[at * 320 : at * 320 + 320, :] = rows
        else:
            distant[...] = rows
    near_t[...] = near[...].astype(F32).T.astype(BF)
    distant_t[...] = distant[...].astype(F32).T.astype(BF)


def prepare(token, scalars, saved):
    _, rows, hidden = saved.shape
    shapes = [(n, hidden)[::turn] for n in (rows, rows * 3 // 4, rows // 4) for turn in (1, -1)]
    return call(
        prepare_kernel, token, [saved], [pl.BlockSpec(saved.shape, lambda j, s: (0, 0, 0))],
        [jax.ShapeDtypeStruct(sh, BF) for sh in shapes],
        [pl.BlockSpec(sh, lambda j, s: (0, 0)) for sh in shapes],
        (1,), 0.1, scalars=scalars,
    )


def picked(meta, rows_of, rows):
    routes, places = positions(meta)
    total = jnp.zeros((rows, meta.shape[1]), F32)
    wanted = lax.broadcasted_iota(I32, total.shape, 0)
    for k in range(TOP):
        row = rows_of(routes[k], places[k])
        total = total + jnp.where(wanted == row, meta[TOP + k : TOP + k + 1, :], 0.0)
    return total.astype(BF), routes, places


def first_pick_kernel(
    scalars, routes, gates, routes_other, gates_other, tokens, tokens_other, out, table, meta, matrix
):
    core = scalars[2]
    count = meta.shape[1]

    @pl.when(pl.program_id(0) == 0)
    def _():
        for s, pair in enumerate(((routes, gates), (routes_other, gates_other))):
            both = jnp.concatenate([x[...].astype(F32) for x in pair], axis=0)
            source = core if s == 0 else 1 - core

            def rows_of(r, place):
                row = ((r >> 2) & 15) * 40 + (r >> 6) * 20 + source * CAP + place
                return jnp.where((r & 3) == 2 * core + 1, row, -1)

            picks, named, places = picked(both, rows_of, out.shape[0])
            matrix[:, s * count : (s + 1) * count] = picks
            if s == 0:
                meta[...] = both
                for k in range(TOP):
                    r = named[k]
                    device = ((r >> 1) & 31) * 4 + (r >> 6) * 2
                    table[k : k + 1, :] = (device + (r & 1)) * CAP + places[k]

    lines = jnp.concatenate([tokens[...], tokens_other[...]], axis=0)
    out[...] = dot(matrix[...], lines).astype(BF)


def first_pick(scalars, slots, slots_other, tokens, tokens_other):
    count, width = tokens.shape
    wide = width // 2
    small = [*slots, *slots_other]
    shapes = [((640, width), BF), ((TOP, count), I32), ((2 * TOP, count), F32)]
    return call(
        first_pick_kernel, None, [*small, tokens, tokens_other],
        [pl.BlockSpec(x.shape, lambda j, s: (0, 0)) for x in small]
        + [pl.BlockSpec((count, wide), lambda j, s: (0, j))] * 2,
        [jax.ShapeDtypeStruct(*sh) for sh in shapes],
        [pl.BlockSpec((640, wide), lambda j, s: (0, j))]
        + [pl.BlockSpec(sh[0], lambda j, s: (0, 0)) for sh in shapes[1:]],
        (2,), 0.1, scratch=[pltpu.VMEM((640, 2 * count), BF)], scalars=scalars,
    )


def line_picker_kernel(scalars, *refs):
    metas, (first, last) = refs[:4], refs[4:]
    count = metas[0].shape[1]
    for s in range(4):
        source = (scalars[0] + 4 - s) & 3

        def rows_of(r, place, low, high, at):
            mine = ((r >> 6) == scalars[1]) & ((r & 1) == 0) & (place >= low) & (place < high)
            return jnp.where(mine, ((r >> 1) & 31) * 8 + at + place - low, -1)

        meta = metas[s][...]
        routes, places = positions(meta)
        wanted = lax.broadcasted_iota(I32, (256, count), 0)
        for out, low, high, at in ((first, 0, 8, 0), (last, 8, CAP, source * 2)):
            total = jnp.zeros((256, count), F32)
            for k in range(TOP):
                row = rows_of(routes[k], places[k], low, high, at)
                total = total + jnp.where(wanted == row, meta[TOP + k : TOP + k + 1, :], 0.0)
            out[:, s * count : (s + 1) * count] = total.astype(BF)


def line_picker(token, scalars, metas):
    count = metas[0].shape[1]
    shape = (256, 4 * count)
    return call(
        line_picker_kernel, token, metas,
        [pl.BlockSpec(x.shape, lambda j, s: (0, 0)) for x in metas],
        [jax.ShapeDtypeStruct(shape, BF)] * 2, [pl.BlockSpec(shape, lambda j, s: (0, 0))] * 2,
        (1,), 0.1, scalars=scalars,
    )


def line_pick_kernel(scalars, first, last, here, down, far_left, far_right, up, out):
    count = here.shape[0]
    left = pl.program_id(0) < pl.num_programs(0) // 2
    far = jnp.where(left, far_left[...], far_right[...])
    tokens = [here[...], down[...], far, up[...]]

    def grouped(rows):
        return rows.reshape(32, 8, rows.shape[1]).astype(BF)

    for s in range(4):
        source = (scalars[0] + 4 - s) & 3
        out[:, source] = grouped(dot(first[:, s * count : (s + 1) * count], tokens[s]))
    out[:, 4] = grouped(dot(last[...], jnp.concatenate(tokens, axis=0)))


def line_pick(token, scalars, matrices, here, down, far, up, block):
    count, width = here.shape
    half = width // block // 2
    every = pl.BlockSpec((count, block), lambda j, s: (0, j))
    (out,), token = call(
        line_pick_kernel, token, [*matrices, here, down, *far, up],
        [pl.BlockSpec(m.shape, lambda j, s: (0, 0)) for m in matrices]
        + [
            every, every,
            pl.BlockSpec((count, block), lambda j, s: (0, jnp.minimum(j, half - 1))),
            pl.BlockSpec((count, block), lambda j, s: (0, jnp.maximum(j - half, 0))),
            every,
        ],
        [jax.ShapeDtypeStruct((32, 5, 8, width), BF)],
        [pl.BlockSpec((32, 5, 8, block), lambda j, s: (0, 0, 0, j))],
        (2 * half,), 0.1, scalars=scalars,
    )
    return out, token


def part_kernel(other, scalars, got, *refs):
    picker = refs[-1]
    layer = 1 - scalars[1] if other else scalars[1]

    @pl.when(pl.program_id(0) == 0)
    def _():
        row = lax.broadcasted_iota(I32, (160, 1), 0)
        source = lax.broadcasted_iota(I32, (160, 320), 1)
        picker[...] = (source == row + (row // 20 + layer) * 20).astype(F32).astype(BF)

    def write(out):
        for half in range(2):
            rows = dot(picker[...], got[half * 320 : half * 320 + 320, :])
            out[half * 160 : half * 160 + 160, :] = rows.astype(BF)

    if other:
        write(refs[-3])
    else:
        for side in range(2):
            pl.when(pl.program_id(0) == side)(functools.partial(write, refs[side]))


def part(token, scalars, got, carried=None):
    width = got.shape[1]
    wide = width // 2
    if carried is None:
        args, specs, aliases = [got], [], {}
        shapes = [(320, wide)] * 2
        out_specs = [pl.BlockSpec((320, wide), lambda j, s: (0, 0))] * 2
    else:
        args, specs, aliases = [got, carried], [pl.BlockSpec(memory_space=pl.ANY)], {2: 1}
        shapes = [(320, width), carried.shape]
        out_specs = [pl.BlockSpec((320, wide), lambda j, s: (0, j)), *specs]
    return call(
        functools.partial(part_kernel, carried is not None), token, args,
        [pl.BlockSpec((640, wide), lambda j, s: (0, j)), *specs],
        [jax.ShapeDtypeStruct(sh, BF) for sh in shapes], out_specs,
        (2,), 0.1, scratch=[pltpu.VMEM((160, 320), BF)], scalars=scalars, aliases=aliases,
    )


def hold(token, carried, after):
    anywhere = [pl.BlockSpec(memory_space=pl.ANY)] * len(carried)
    return call(
        lambda *refs: None, token, carried, anywhere,
        [jax.ShapeDtypeStruct(x.shape, x.dtype) for x in carried], anywhere, (1,), 0.1,
        aliases={n: n for n in range(len(carried))}, after=after,
    )


def lines_of(rows):
    blocks = [r[...] for r in rows]
    if len(blocks) > 1:
        blocks = [jnp.where(pl.program_id(0) == 0, blocks[0], blocks[1]), *blocks[2:]]
    return jnp.concatenate(blocks, axis=0)


def line_specs(rows, wide):
    return [
        pl.BlockSpec((r.shape[0], wide), (lambda j: (0, 0)) if r.shape[1] == wide else (lambda j: (0, j)))
        for r in rows
    ]


def close(total, saved, hidden, terms):
    hidden[...] = total[...].astype(BF)
    products = saved[...].astype(F32) * total[...]
    lanes = sum(products[:, at : at + 128] for at in range(0, products.shape[1], 128))
    terms[...] = jnp.sum(lanes.T, axis=0, keepdims=True)


def back_kernel(pieces, *refs):
    rows, (weight, saved, hidden, terms, total) = refs[:pieces], refs[pieces:]

    @pl.when(pl.program_id(0) == 0)
    def _():
        total[...] = jnp.zeros_like(total)

    total[...] += lax.dot_general(
        lines_of(rows), weight[...], (((1,), (1,)), ((), ())), preferred_element_type=F32
    )
    pl.when(pl.program_id(0) == 1)(functools.partial(close, total, saved, hidden, terms))


def back(token, rows, weight, saved, expert):
    shape = saved.shape
    wide = weight.shape[2] // 2
    whole = pl.BlockSpec(shape, lambda j: (0, 0))
    return call(
        functools.partial(back_kernel, len(rows)), token, [*rows, weight, saved],
        line_specs(rows, wide)
        + [pl.BlockSpec((None, shape[1], wide), lambda j: (expert, 0, j)), whole],
        [jax.ShapeDtypeStruct(shape, BF), jax.ShapeDtypeStruct((1, shape[0]), F32)],
        [whole, pl.BlockSpec((1, shape[0]), lambda j: (0, 0))],
        (2,), 0.1, scratch=[pltpu.VMEM(shape, F32)],
    )


def down_kernel(pieces, saved_t, *refs):
    refs[pieces][...] = dot(saved_t[...], lines_of(refs[:pieces]))


def down(token, saved_t, rows, width):
    hidden = saved_t.shape[0]
    wide = width // 2
    (out,), token = call(
        functools.partial(down_kernel, len(rows)), token, [saved_t, *rows],
        [pl.BlockSpec(saved_t.shape, lambda j: (0, 0)), *line_specs(rows, wide)],
        [jax.ShapeDtypeStruct((hidden, width), F32)],
        [pl.BlockSpec((hidden, wide), lambda j: (0, j))], (2,), 0.1,
    )
    return out, token


def distant_kernel(last, rows, weight, saved_t, before, *refs):
    if last:
        so_far, saved, _, out, hidden, terms, total = refs
    else:
        out, total = refs
    out[...] = (dot(saved_t[...], rows[...]) + before[...]).astype(BF)

    @pl.when(pl.program_id(0) == 0)
    def _():
        total[...] = so_far[...] if last else jnp.zeros_like(total)

    total[...] += lax.dot_general(
        rows[...], weight[...], (((1,), (1,)), ((), ())), preferred_element_type=F32
    )
    if last:
        pl.when(pl.program_id(0) == 1)(functools.partial(close, total, saved, hidden, terms))


def distant_rows(token, rows, weight, saved, saved_t, before, earlier=None):
    size, wide = rows.shape
    hidden = saved.shape[1]
    block = wide // 2
    last = earlier is not None
    side = 2 * last
    whole = pl.BlockSpec(saved.shape, lambda j: (0, 0))
    out = jax.ShapeDtypeStruct((2, hidden, 2 * wide), BF)
    total = jax.ShapeDtypeStruct(saved.shape, F32)
    args = [rows, weight, saved_t, before]
    specs = [
        pl.BlockSpec((size, block), lambda j: (0, j)),
        pl.BlockSpec((None, hidden, block), lambda j: (1, 0, j + side)),
        pl.BlockSpec(saved_t.shape, lambda j: (0, 0)),
        pl.BlockSpec((hidden, block), lambda j: (0, j + side)),
    ]
    out_specs = [pl.BlockSpec((None, hidden, block), lambda j: (1, 0, j + side))]
    if last:
        args += [earlier[1], saved, earlier[0]]
        specs += [whole, whole, pl.BlockSpec(memory_space=pl.ANY)]
        shapes = [out, jax.ShapeDtypeStruct(saved.shape, BF), jax.ShapeDtypeStruct((1, size), F32)]
        out_specs += [whole, pl.BlockSpec((1, size), lambda j: (0, 0))]
    else:
        shapes = [out, total]
        out_specs.append(whole)
    return call(
        functools.partial(distant_kernel, last), token, args, specs, shapes, out_specs,
        (2,), 0.1, scratch=[pltpu.VMEM(saved.shape, F32)] if last else [],
        aliases={6: 0} if last else {},
    )


def finish_kernel(scalars, saved_t, rows, hidden0, near, distant, _, down_out, hidden_out):
    down_out[...] = dot(saved_t[...], rows[...]).astype(BF)

    @pl.when(pl.program_id(0) == 0)
    def _():
        row = lax.broadcasted_iota(I32, (160, 1), 0)
        plane, place = row // CAP, row % CAP
        source = lax.broadcasted_iota(I32, (160, 640), 1)
        for z in range(4):
            line = jnp.where(place < 8, z * 8 + place, 24 + z * 2 + place)
            hit = (source == plane * 40 + line).astype(F32).astype(BF)
            for half in range(2):
                lines = dot(hit, hidden0[half * 640 : half * 640 + 640, :])
                at = z * 320 + half * 160
                hidden_out[0, at : at + 160, :] = lines.astype(BF)
        for at, step in enumerate(STEPS):
            begin = pl.multiple_of(((scalars[0] + 4 - step) & 3) * 320, 320)
            hidden_out[1, pl.ds(begin, 320), :] = (
                near[at * 320 : at * 320 + 320, :] if at < 3 else distant[...]
            )


def finish(token, scalars, saved_t, rows, hidden0, near, distant, result):
    count, width = rows.shape
    hidden = saved_t.shape[0]
    wide = width // 2
    args = [saved_t, rows, hidden0, near, distant, result]
    specs = [pl.BlockSpec(x.shape, lambda j, s: (0, 0)) for x in args[:-1]]
    specs[1] = pl.BlockSpec((count, wide), lambda j, s: (0, j))
    shape = (2, count, hidden)
    outs, _ = call(
        finish_kernel, token, args, [*specs, pl.BlockSpec(memory_space=pl.ANY)],
        [jax.ShapeDtypeStruct(result.shape, BF), jax.ShapeDtypeStruct(shape, BF)],
        [
            pl.BlockSpec((None, hidden, wide), lambda j, s: (0, 0, j)),
            pl.BlockSpec(shape, lambda j, s: (0, 0, 0)),
        ],
        (2,), 0.1, scalars=scalars, aliases={len(args): 0},
    )
    return outs


def shards(grad_out, gates, routes, w_down, saved_hidden):
    tokens, width = grad_out.shape
    zh, zl = lax.axis_index("zh"), lax.axis_index("zl")
    core = lax.axis_index("core")
    z = zh * 2 + zl
    scalars = jnp.stack([z, zl, core]).astype(I32)

    wide = width // 2

    from_down, from_up = z_shift(grad_out, 1), z_shift(grad_out, -1)
    slots = (routes.T, gates.T)
    other = core_swap(grad_out)
    (send1, table, meta), token = first_pick(
        scalars, slots, [core_swap(x) for x in slots], grad_out, other
    )
    got1 = lax.all_to_all(send1.reshape(16, 40, width), ("y", "x"), 0, 0, tiled=True)
    got1 = got1.reshape(640, width)

    (onward_down, onward_up, meta), token = onward(token, from_down, from_up, meta, wide)
    metas = [meta, z_shift(meta, 1), z_shift(meta, 2), z_shift(meta, -1)]
    far = (z_shift(onward_down, 1), z_shift(onward_up, -1))
    saved, token = prepare(token, scalars, saved_hidden)
    saved0, saved0_t, saved_near, saved_near_t, saved_distant, saved_distant_t = saved
    matrices, token = line_picker(token, scalars, metas)

    send0, token = line_pick(
        token, scalars, matrices, grad_out, from_down, far, from_up, width // 4
    )
    (away, send0), token = part(token, scalars, got1, send0)
    rows0 = lax.all_to_all(send0, PLANE, 0, 0, tiled=True).reshape(1280, width)
    near = [z_shift(away, 1), z_shift(away, -1)]
    own, token = part(token, scalars, got1)
    own, token = hold(token, own, near)
    near = [*own, *near]
    distant = [z_shift(half, 2) for half in own]

    (hidden_near, terms_near), token = back(token, near, w_down, saved_near, 1)
    before, token = down(token, saved_near_t, near, width)
    more = (w_down, saved_distant, saved_distant_t, before)
    earlier, token = distant_rows(token, distant[0], *more)
    (d_down, hidden_distant, terms_distant), token = distant_rows(
        token, distant[1], *more, earlier
    )
    (hidden0, terms0), token = back(token, [rows0], w_down, saved0, 0)
    d_down, d_hidden = finish(
        token, scalars, saved0_t, rows0, hidden0, hidden_near, hidden_distant, d_down
    )

    terms_near = terms_near.reshape(3, 32, CAP)
    terms1 = jnp.stack(
        [terms_near[0], terms_near[1], terms_distant.reshape(32, CAP), terms_near[2]], axis=1
    )
    terms1 = jnp.concatenate(
        [lax.dynamic_index_in_dim(terms1, (z - i) % 4, 1, True) for i in range(4)], axis=1
    )
    terms0 = terms0.reshape(32, 40)
    terms0 = jnp.concatenate(
        [terms0[:, :32].reshape(32, 4, 8), terms0[:, 32:].reshape(32, 4, 2)], axis=2
    )
    terms = jnp.concatenate([terms0, terms1], axis=2).reshape(128, 2 * CAP)
    returned = lax.all_to_all(terms, PLANE + Z, 0, 0, tiled=True)
    returned = returned.reshape(32, 2, 2, 2 * CAP)
    returned = (returned[:, 0] + returned[:, 1]).reshape(-1)

    table = table.reshape(1, -1)
    d_gates = jnp.sum(
        jnp.where(
            table == jnp.arange(EXPERTS * CAP, dtype=I32)[:, None], returned[:, None], 0.0
        ),
        axis=0,
    ).reshape(TOP, tokens).T
    return d_gates / gates.astype(F32), d_down, d_hidden


def solution(mesh):
    fine = Mesh(mesh.devices.reshape(2, 2, 4, 4, 2), ALL)
    in_specs = (
        P(ALL, None),
        P(ALL, None),
        P(ALL, None),
        P(("zl", "y", "x", "core"), "zh", None),
        P(("zl", "y", "x", "core"), None, "zh"),
    )
    out_specs = (P(ALL, None), in_specs[3], in_specs[4])
    return jax.shard_map(shards, mesh=fine, in_specs=in_specs, out_specs=out_specs, check_vma=False)
```

```python
import functools

import jax
import jax.numpy as jnp
from jax import lax
from jax.experimental import pallas as pl
from jax.experimental.pallas import tpu as pltpu
from jax.sharding import Mesh, PartitionSpec as P

Z = ("zh", "zl")
PLANE = ("y", "x", "core")
ALL = ("zh", "zl", "y", "x", "core")
CAP = 10
LATE = 46
TOP = 4
STEPS = (0, 1, 3, 2)
EXPERTS = 128
BF = jnp.bfloat16
F32 = jnp.float32
I32 = jnp.int32


def z_shift(value, step):
    return lax.ppermute(value, Z, [(i, (i + step) % 4) for i in range(4)])


def core_swap(value):
    return lax.ppermute(value, "core", [(0, 1), (1, 0)])


def dot(a, b):
    return jnp.dot(a, b, preferred_element_type=F32)


def call(body, token, args, in_specs, out_shape, out_specs, grid, micros, scratch=(), aliases=None,
         scalars=None, after=(), limit=60):
    lead = 0 if scalars is None else 1
    extra = [*([] if token is None else [token]), *after]
    n_in, n_out = lead + len(args), len(out_shape)

    def run(*refs):
        outs = refs[n_in + len(extra) :]
        outs[n_out][...] = jnp.zeros((8, 128), F32)
        body(*refs[:n_in], *outs[:n_out], *outs[n_out + 1 :])

    result = pl.pallas_call(
        run,
        out_shape=[*out_shape, jax.ShapeDtypeStruct((8, 128), F32)],
        grid_spec=pltpu.PrefetchScalarGridSpec(
            num_scalar_prefetch=lead,
            grid=grid,
            in_specs=[*in_specs, *[pl.BlockSpec(memory_space=pl.ANY)] * len(extra)],
            out_specs=[*out_specs, pl.BlockSpec((8, 128), lambda j, *_: (0, 0))],
            scratch_shapes=list(scratch),
        ),
        input_output_aliases=aliases or {},
        compiler_params=pltpu.CompilerParams(vmem_limit_bytes=limit * 1024 * 1024),
        cost_estimate=pl.CostEstimate(
            flops=int(micros * 1e9), bytes_accessed=0, transcendentals=0
        ),
    )(*([] if scalars is None else [scalars]), *args, *extra)
    return result[:-1], result[-1]


def positions(meta):
    tokens = meta.shape[1]
    names = lax.broadcasted_iota(I32, (EXPERTS, tokens), 0)
    routes = [meta[k : k + 1, :].astype(I32) for k in range(TOP)]
    hits = [names == r for r in routes]
    named = sum(h.astype(F32) for h in hits)
    first = lax.broadcasted_iota(I32, (tokens, tokens), 0)
    second = lax.broadcasted_iota(I32, (tokens, tokens), 1)
    earlier = dot(named.astype(BF), (first < second).astype(F32).astype(BF))
    places = [
        jnp.sum(jnp.where(h, earlier, 0.0), axis=0, keepdims=True).astype(I32) for h in hits
    ]
    return routes, places


def onward_kernel(below, above, meta, down, up, meta_out):
    cut = down.shape[1]
    down[...] = below[:, :cut]
    up[...] = above[:, cut:]
    meta_out[...] = meta[...]


def onward(token, from_down, from_up, meta, cut):
    rows, width = from_down.shape
    shapes = [((rows, cut), BF), ((rows, width - cut), BF), (meta.shape, F32)]
    return call(
        onward_kernel, token, [from_down, from_up, meta],
        [
            pl.BlockSpec((rows, cut), lambda j: (0, 0)),
            pl.BlockSpec((rows, width), lambda j: (0, 0)),
            pl.BlockSpec(meta.shape, lambda j: (0, 0)),
        ],
        [jax.ShapeDtypeStruct(*sh) for sh in shapes],
        [pl.BlockSpec(sh[0], lambda j: (0, 0)) for sh in shapes], (1,), 1000,
    )


def prepare_kernel(scalars, saved, saved0, saved0_t, near, near_t, distant, distant_t):
    row = lax.broadcasted_iota(I32, (320, 1), 0)
    source = lax.broadcasted_iota(I32, (320, 1280), 1)
    for q in range(4):
        at = row + q * 320
        plane, line = at // 40, at % 40
        z = jnp.where(line < 32, line // 8, (line - 32) // 2)
        place = jnp.where(line < 32, line % 8, 8 + line % 2)
        hit = (source == z * 320 + plane * CAP + place).astype(F32).astype(BF)
        rows = dot(hit, saved[0])
        saved0[q * 320 : q * 320 + 320, :] = rows.astype(BF)
    saved0_t[...] = saved0[...].astype(F32).T.astype(BF)
    for at, step in enumerate(STEPS):
        begin = pl.multiple_of(((scalars[0] + 4 - step) & 3) * 320, 320)
        rows = saved[1, pl.ds(begin, 320), :]
        if at < 3:
            near[at * 320 : at * 320 + 320, :] = rows
        else:
            distant[...] = rows
    near_t[...] = near[...].astype(F32).T.astype(BF)
    distant_t[...] = distant[...].astype(F32).T.astype(BF)


def prepare(token, scalars, saved):
    _, rows, hidden = saved.shape
    shapes = [(n, hidden)[::turn] for n in (rows, rows * 3 // 4, rows // 4) for turn in (1, -1)]
    return call(
        prepare_kernel, token, [saved], [pl.BlockSpec(saved.shape, lambda j, s: (0, 0, 0))],
        [jax.ShapeDtypeStruct(sh, BF) for sh in shapes],
        [pl.BlockSpec(sh, lambda j, s: (0, 0)) for sh in shapes],
        (1,), 0.1, scalars=scalars,
    )


def picked(meta, rows_of, rows):
    routes, places = positions(meta)
    total = jnp.zeros((rows, meta.shape[1]), F32)
    wanted = lax.broadcasted_iota(I32, total.shape, 0)
    for k in range(TOP):
        row = rows_of(routes[k], places[k])
        total = total + jnp.where(wanted == row, meta[TOP + k : TOP + k + 1, :], 0.0)
    return total.astype(BF), routes, places


def first_pick_kernel(
    scalars, routes, gates, routes_other, gates_other, tokens, tokens_other, out, table, meta, matrix
):
    core = scalars[2]
    count = meta.shape[1]

    @pl.when(pl.program_id(0) == 0)
    def _():
        for s, pair in enumerate(((routes, gates), (routes_other, gates_other))):
            both = jnp.concatenate([x[...].astype(F32) for x in pair], axis=0)
            source = core if s == 0 else 1 - core

            def rows_of(r, place):
                row = ((r >> 2) & 15) * 40 + (r >> 6) * 20 + source * CAP + place
                return jnp.where((r & 3) == 2 * core + 1, row, -1)

            picks, named, places = picked(both, rows_of, out.shape[0])
            matrix[:, s * count : (s + 1) * count] = picks
            if s == 0:
                meta[...] = both
                for k in range(TOP):
                    r = named[k]
                    device = ((r >> 1) & 31) * 4 + (r >> 6) * 2
                    table[k : k + 1, :] = (device + (r & 1)) * CAP + places[k]

    lines = jnp.concatenate([tokens[...], tokens_other[...]], axis=0)
    out[...] = dot(matrix[...], lines).astype(BF)


def first_pick(scalars, slots, slots_other, tokens, tokens_other):
    count, width = tokens.shape
    wide = width // 2
    small = [*slots, *slots_other]
    shapes = [((640, width), BF), ((TOP, count), I32), ((2 * TOP, count), F32)]
    return call(
        first_pick_kernel, None, [*small, tokens, tokens_other],
        [pl.BlockSpec(x.shape, lambda j, s: (0, 0)) for x in small]
        + [pl.BlockSpec((count, wide), lambda j, s: (0, j))] * 2,
        [jax.ShapeDtypeStruct(*sh) for sh in shapes],
        [pl.BlockSpec((640, wide), lambda j, s: (0, j))]
        + [pl.BlockSpec(sh[0], lambda j, s: (0, 0)) for sh in shapes[1:]],
        (2,), 0.1, scratch=[pltpu.VMEM((640, 2 * count), BF)], scalars=scalars,
    )


def line_picker_kernel(scalars, *refs):
    metas, (first, last) = refs[:4], refs[4:]
    count = metas[0].shape[1]
    for s in range(4):
        source = (scalars[0] + 4 - s) & 3

        def rows_of(r, place, low, high, at):
            mine = ((r >> 6) == scalars[1]) & ((r & 1) == 0) & (place >= low) & (place < high)
            return jnp.where(mine, ((r >> 1) & 31) * 8 + at + place - low, -1)

        meta = metas[s][...]
        routes, places = positions(meta)
        wanted = lax.broadcasted_iota(I32, (256, count), 0)
        for out, low, high, at in ((first, 0, 8, 0), (last, 8, CAP, source * 2)):
            total = jnp.zeros((256, count), F32)
            for k in range(TOP):
                row = rows_of(routes[k], places[k], low, high, at)
                total = total + jnp.where(wanted == row, meta[TOP + k : TOP + k + 1, :], 0.0)
            out[:, s * count : (s + 1) * count] = total.astype(BF)


def line_picker(token, scalars, metas):
    count = metas[0].shape[1]
    shape = (256, 4 * count)
    return call(
        line_picker_kernel, token, metas,
        [pl.BlockSpec(x.shape, lambda j, s: (0, 0)) for x in metas],
        [jax.ShapeDtypeStruct(shape, BF)] * 2, [pl.BlockSpec(shape, lambda j, s: (0, 0))] * 2,
        (1,), 0.1, scalars=scalars,
    )


def line_pick_kernel(scalars, first, last, here, down, far_left, far_right, up, out):
    count = here.shape[0]
    left = pl.program_id(0) < pl.num_programs(0) // 2
    far = jnp.where(left, far_left[...], far_right[...])
    tokens = [here[...], down[...], far, up[...]]

    def grouped(rows):
        return rows.reshape(32, 8, rows.shape[1]).astype(BF)

    for s in range(4):
        source = (scalars[0] + 4 - s) & 3
        out[:, source] = grouped(dot(first[:, s * count : (s + 1) * count], tokens[s]))
    out[:, 4] = grouped(dot(last[...], jnp.concatenate(tokens, axis=0)))


def line_pick(token, scalars, matrices, here, down, far, up, block):
    count, width = here.shape
    half = width // block // 2
    every = pl.BlockSpec((count, block), lambda j, s: (0, j))
    (out,), token = call(
        line_pick_kernel, token, [*matrices, here, down, *far, up],
        [pl.BlockSpec(m.shape, lambda j, s: (0, 0)) for m in matrices]
        + [
            every, every,
            pl.BlockSpec((count, block), lambda j, s: (0, jnp.minimum(j, half - 1))),
            pl.BlockSpec((count, block), lambda j, s: (0, jnp.maximum(j - half, 0))),
            every,
        ],
        [jax.ShapeDtypeStruct((32, 5, 8, width), BF)],
        [pl.BlockSpec((32, 5, 8, block), lambda j, s: (0, 0, 0, j))],
        (2 * half,), 0.1, scalars=scalars,
    )
    return out, token


def part_kernel(other, scalars, got, out, *refs):
    picker = refs[-1]
    layer = 1 - scalars[1] if other else scalars[1]

    @pl.when(pl.program_id(0) == 0)
    def _():
        row = lax.broadcasted_iota(I32, (160, 1), 0)
        source = lax.broadcasted_iota(I32, (160, 320), 1)
        picker[...] = (source == row + (row // 20 + layer) * 20).astype(F32).astype(BF)

    for half in range(2):
        rows = dot(picker[...], got[half * 320 : half * 320 + 320, :])
        out[half * 160 : half * 160 + 160, :] = rows.astype(BF)
    if not other:
        left, right = refs[:2]
        wide, rest = out.shape[1], right.shape[1]

        @pl.when(pl.program_id(0) == 0)
        def _():
            left[:, :wide] = out[...]

        @pl.when(pl.program_id(0) == 1)
        def _():
            left[:, wide:] = out[:, : wide - rest]
            right[...] = out[:, wide - rest :]


def part(token, scalars, got, other):
    width = got.shape[1]
    wide = width // 2
    shapes = [(320, width)] + [(320, width * n // 4) for n in (3, 1)] * (not other)
    return call(
        functools.partial(part_kernel, other), token, [got],
        [pl.BlockSpec((640, wide), lambda j, s: (0, j))],
        [jax.ShapeDtypeStruct(sh, BF) for sh in shapes],
        [pl.BlockSpec((320, wide), lambda j, s: (0, j))]
        + [pl.BlockSpec(sh, lambda j, s: (0, 0)) for sh in shapes[1:]],
        (2,), 0.1, scratch=[pltpu.VMEM((160, 320), BF)], scalars=scalars,
        limit=60 if other else LATE,
    )


def hold(token, carried, after):
    anywhere = [pl.BlockSpec(memory_space=pl.ANY)] * len(carried)
    return call(
        lambda *refs: None, token, carried, anywhere,
        [jax.ShapeDtypeStruct(x.shape, x.dtype) for x in carried], anywhere, (1,), 0.1,
        aliases={n: n for n in range(len(carried))}, after=after, limit=LATE,
    )


def lines_of(rows):
    return jnp.concatenate([r[...] for r in rows], axis=0)


def line_specs(rows, wide):
    return [pl.BlockSpec((r.shape[0], wide), lambda j: (0, j)) for r in rows]


def close(total, saved, hidden, terms):
    hidden[...] = total[...].astype(BF)
    products = saved[...].astype(F32) * total[...]
    lanes = sum(products[:, at : at + 128] for at in range(0, products.shape[1], 128))
    terms[...] = jnp.sum(lanes.T, axis=0, keepdims=True)


def back_kernel(pieces, *refs):
    rows, (weight, saved, hidden, terms, total) = refs[:pieces], refs[pieces:]

    @pl.when(pl.program_id(0) == 0)
    def _():
        total[...] = jnp.zeros_like(total)

    total[...] += lax.dot_general(
        lines_of(rows), weight[...], (((1,), (1,)), ((), ())), preferred_element_type=F32
    )
    pl.when(pl.program_id(0) == 1)(functools.partial(close, total, saved, hidden, terms))


def back(token, rows, weight, saved, expert):
    shape = saved.shape
    wide = weight.shape[2] // 2
    whole = pl.BlockSpec(shape, lambda j: (0, 0))
    return call(
        functools.partial(back_kernel, len(rows)), token, [*rows, weight, saved],
        line_specs(rows, wide)
        + [pl.BlockSpec((None, shape[1], wide), lambda j: (expert, 0, j)), whole],
        [jax.ShapeDtypeStruct(shape, BF), jax.ShapeDtypeStruct((1, shape[0]), F32)],
        [whole, pl.BlockSpec((1, shape[0]), lambda j: (0, 0))],
        (2,), 0.1, limit=LATE, scratch=[pltpu.VMEM(shape, F32)],
    )


def down_kernel(pieces, saved_t, *refs):
    refs[pieces][...] = dot(saved_t[...], lines_of(refs[:pieces]))


def down(token, saved_t, rows, width):
    hidden = saved_t.shape[0]
    wide = width // 2
    (out,), token = call(
        functools.partial(down_kernel, len(rows)), token, [saved_t, *rows],
        [pl.BlockSpec(saved_t.shape, lambda j: (0, 0)), *line_specs(rows, wide)],
        [jax.ShapeDtypeStruct((hidden, width), F32)],
        [pl.BlockSpec((hidden, wide), lambda j: (0, j))], (2,), 0.1, limit=LATE,
    )
    return out, token


def distant_kernel(last, rows, weight, saved_t, before, *refs):
    if last:
        so_far, saved, _, out, hidden, terms, total = refs
    else:
        out, total = refs
    out[...] = (dot(saved_t[...], rows[...]) + before[...]).astype(BF)

    @pl.when(pl.program_id(0) == 0)
    def _():
        total[...] = so_far[...] if last else jnp.zeros_like(total)

    total[...] += lax.dot_general(
        rows[...], weight[...], (((1,), (1,)), ((), ())), preferred_element_type=F32
    )
    if last:
        close(total, saved, hidden, terms)


def distant_rows(token, rows, weight, saved, saved_t, before, earlier=None):
    (hidden, width), size = before.shape, rows.shape[0]
    block = width // 4
    last = earlier is not None
    side = 3 * last
    whole = pl.BlockSpec(saved.shape, lambda j: (0, 0))
    out = jax.ShapeDtypeStruct((2, hidden, width), BF)
    total = jax.ShapeDtypeStruct(saved.shape, F32)
    args = [rows, weight, saved_t, before]
    specs = [
        pl.BlockSpec((size, block), lambda j: (0, j)),
        pl.BlockSpec((None, hidden, block), lambda j: (1, 0, j + side)),
        pl.BlockSpec(saved_t.shape, lambda j: (0, 0)),
        pl.BlockSpec((hidden, block), lambda j: (0, j + side)),
    ]
    out_specs = [pl.BlockSpec((None, hidden, block), lambda j: (1, 0, j + side))]
    if last:
        args += [earlier[1], saved, earlier[0]]
        specs += [whole, whole, pl.BlockSpec(memory_space=pl.ANY)]
        shapes = [out, jax.ShapeDtypeStruct(saved.shape, BF), jax.ShapeDtypeStruct((1, size), F32)]
        out_specs += [whole, pl.BlockSpec((1, size), lambda j: (0, 0))]
    else:
        shapes = [out, total]
        out_specs.append(whole)
    return call(
        functools.partial(distant_kernel, last), token, args, specs, shapes, out_specs,
        (rows.shape[1] // block,), 0.1, limit=LATE, scratch=[pltpu.VMEM(saved.shape, F32)] if last else [],
        aliases={6: 0} if last else {},
    )


def finish_kernel(scalars, saved_t, rows, hidden0, near, distant, _, down_out, hidden_out):
    down_out[...] = dot(saved_t[...], rows[...]).astype(BF)

    @pl.when(pl.program_id(0) == 0)
    def _():
        row = lax.broadcasted_iota(I32, (160, 1), 0)
        plane, place = row // CAP, row % CAP
        source = lax.broadcasted_iota(I32, (160, 640), 1)
        for z in range(4):
            line = jnp.where(place < 8, z * 8 + place, 24 + z * 2 + place)
            hit = (source == plane * 40 + line).astype(F32).astype(BF)
            for half in range(2):
                lines = dot(hit, hidden0[half * 640 : half * 640 + 640, :])
                at = z * 320 + half * 160
                hidden_out[0, at : at + 160, :] = lines.astype(BF)
        for at, step in enumerate(STEPS):
            begin = pl.multiple_of(((scalars[0] + 4 - step) & 3) * 320, 320)
            hidden_out[1, pl.ds(begin, 320), :] = (
                near[at * 320 : at * 320 + 320, :] if at < 3 else distant[...]
            )


def finish(token, scalars, saved_t, rows, hidden0, near, distant, result):
    count, width = rows.shape
    hidden = saved_t.shape[0]
    wide = width // 2
    args = [saved_t, rows, hidden0, near, distant, result]
    specs = [pl.BlockSpec(x.shape, lambda j, s: (0, 0)) for x in args[:-1]]
    specs[1] = pl.BlockSpec((count, wide), lambda j, s: (0, j))
    shape = (2, count, hidden)
    outs, _ = call(
        finish_kernel, token, args, [*specs, pl.BlockSpec(memory_space=pl.ANY)],
        [jax.ShapeDtypeStruct(result.shape, BF), jax.ShapeDtypeStruct(shape, BF)],
        [
            pl.BlockSpec((None, hidden, wide), lambda j, s: (0, 0, j)),
            pl.BlockSpec(shape, lambda j, s: (0, 0, 0)),
        ],
        (2,), 0.1, scalars=scalars, aliases={len(args): 0},
    )
    return outs


def shards(grad_out, gates, routes, w_down, saved_hidden):
    tokens, width = grad_out.shape
    zh, zl = lax.axis_index("zh"), lax.axis_index("zl")
    core = lax.axis_index("core")
    z = zh * 2 + zl
    scalars = jnp.stack([z, zl, core]).astype(I32)

    wide = width // 2

    from_down, from_up = z_shift(grad_out, 1), z_shift(grad_out, -1)
    slots = (routes.T, gates.T)
    other = core_swap(grad_out)
    (send1, table, meta), token = first_pick(
        scalars, slots, [core_swap(x) for x in slots], grad_out, other
    )
    got1 = lax.all_to_all(send1.reshape(16, 40, width), ("y", "x"), 0, 0, tiled=True)
    got1 = got1.reshape(640, width)

    (onward_down, onward_up, meta), token = onward(token, from_down, from_up, meta, wide)
    metas = [meta, z_shift(meta, 1), z_shift(meta, 2), z_shift(meta, -1)]
    far = (z_shift(onward_down, 1), z_shift(onward_up, -1))
    saved, token = prepare(token, scalars, saved_hidden)
    saved0, saved0_t, saved_near, saved_near_t, saved_distant, saved_distant_t = saved
    matrices, token = line_picker(token, scalars, metas)

    send0, token = line_pick(
        token, scalars, matrices, grad_out, from_down, far, from_up, width // 4
    )
    (away,), token = part(token, scalars, got1, True)
    rows0 = lax.all_to_all(send0, PLANE, 0, 0, tiled=True).reshape(1280, width)
    near = [z_shift(away, 1), z_shift(away, -1)]
    (own, *own_parts), token = part(token, scalars, got1, False)
    own_parts, token = hold(token, own_parts, near)
    near = [own, *near]
    distant = [z_shift(x, 2) for x in own_parts]

    (hidden_near, terms_near), token = back(token, near, w_down, saved_near, 1)
    before, token = down(token, saved_near_t, near, width)
    more = (w_down, saved_distant, saved_distant_t, before)
    earlier, token = distant_rows(token, distant[0], *more)
    (d_down, hidden_distant, terms_distant), token = distant_rows(
        token, distant[1], *more, earlier
    )
    (hidden0, terms0), token = back(token, [rows0], w_down, saved0, 0)
    d_down, d_hidden = finish(
        token, scalars, saved0_t, rows0, hidden0, hidden_near, hidden_distant, d_down
    )

    terms_near = terms_near.reshape(3, 32, CAP)
    terms1 = jnp.stack(
        [terms_near[0], terms_near[1], terms_distant.reshape(32, CAP), terms_near[2]], axis=1
    )
    terms1 = jnp.concatenate(
        [lax.dynamic_index_in_dim(terms1, (z - i) % 4, 1, True) for i in range(4)], axis=1
    )
    terms0 = terms0.reshape(32, 40)
    terms0 = jnp.concatenate(
        [terms0[:, :32].reshape(32, 4, 8), terms0[:, 32:].reshape(32, 4, 2)], axis=2
    )
    terms = jnp.concatenate([terms0, terms1], axis=2).reshape(128, 2 * CAP)
    returned = lax.all_to_all(terms, PLANE + Z, 0, 0, tiled=True)
    returned = returned.reshape(32, 2, 2, 2 * CAP)
    returned = (returned[:, 0] + returned[:, 1]).reshape(-1)

    table = table.reshape(1, -1)
    d_gates = jnp.sum(
        jnp.where(
            table == jnp.arange(EXPERTS * CAP, dtype=I32)[:, None], returned[:, None], 0.0
        ),
        axis=0,
    ).reshape(TOP, tokens).T
    return d_gates / gates.astype(F32), d_down, d_hidden


def solution(mesh):
    fine = Mesh(mesh.devices.reshape(2, 2, 4, 4, 2), ALL)
    in_specs = (
        P(ALL, None),
        P(ALL, None),
        P(ALL, None),
        P(("zl", "y", "x", "core"), "zh", None),
        P(("zl", "y", "x", "core"), None, "zh"),
    )
    out_specs = (P(ALL, None), in_specs[3], in_specs[4])
    return jax.shard_map(shards, mesh=fine, in_specs=in_specs, out_specs=out_specs, check_vma=False)
```

```python
import functools

import jax
import jax.numpy as jnp
from jax import lax
from jax.experimental import pallas as pl
from jax.experimental.pallas import tpu as pltpu
from jax.sharding import Mesh, PartitionSpec as P

Z = ("zh", "zl")
PLANE = ("y", "x", "core")
ALL = ("zh", "zl", "y", "x", "core")
CAP = 10
LATE = 46
TOP = 4
STEPS = (0, 1, 3, 2)
EXPERTS = 128
BF = jnp.bfloat16
F32 = jnp.float32
I32 = jnp.int32


def z_shift(value, step):
    return lax.ppermute(value, Z, [(i, (i + step) % 4) for i in range(4)])


def core_swap(value):
    return lax.ppermute(value, "core", [(0, 1), (1, 0)])


def dot(a, b):
    return jnp.dot(a, b, preferred_element_type=F32)


def call(body, token, args, in_specs, out_shape, out_specs, grid, micros, scratch=(), aliases=None,
         scalars=None, after=(), limit=60):
    lead = 0 if scalars is None else 1
    extra = [*([] if token is None else [token]), *after]
    n_in, n_out = lead + len(args), len(out_shape)

    def run(*refs):
        outs = refs[n_in + len(extra) :]
        outs[n_out][...] = jnp.zeros((8, 128), F32)
        body(*refs[:n_in], *outs[:n_out], *outs[n_out + 1 :])

    result = pl.pallas_call(
        run,
        out_shape=[*out_shape, jax.ShapeDtypeStruct((8, 128), F32)],
        grid_spec=pltpu.PrefetchScalarGridSpec(
            num_scalar_prefetch=lead,
            grid=grid,
            in_specs=[*in_specs, *[pl.BlockSpec(memory_space=pl.ANY)] * len(extra)],
            out_specs=[*out_specs, pl.BlockSpec((8, 128), lambda j, *_: (0, 0))],
            scratch_shapes=list(scratch),
        ),
        input_output_aliases=aliases or {},
        compiler_params=pltpu.CompilerParams(vmem_limit_bytes=limit * 1024 * 1024),
        cost_estimate=pl.CostEstimate(
            flops=int(micros * 1e9), bytes_accessed=0, transcendentals=0
        ),
    )(*([] if scalars is None else [scalars]), *args, *extra)
    return result[:-1], result[-1]


def positions(meta):
    tokens = meta.shape[1]
    names = lax.broadcasted_iota(I32, (EXPERTS, tokens), 0)
    routes = [meta[k : k + 1, :].astype(I32) for k in range(TOP)]
    hits = [names == r for r in routes]
    named = sum(h.astype(F32) for h in hits)
    first = lax.broadcasted_iota(I32, (tokens, tokens), 0)
    second = lax.broadcasted_iota(I32, (tokens, tokens), 1)
    earlier = dot(named.astype(BF), (first < second).astype(F32).astype(BF))
    places = [
        jnp.sum(jnp.where(h, earlier, 0.0), axis=0, keepdims=True).astype(I32) for h in hits
    ]
    return routes, places


def onward_kernel(below, above, meta, down, up, meta_out):
    cut = down.shape[1]
    down[...] = below[:, :cut]
    up[...] = above[:, cut:]
    meta_out[...] = meta[...]


def onward(token, from_down, from_up, meta, cut):
    rows, width = from_down.shape
    shapes = [((rows, cut), BF), ((rows, width - cut), BF), (meta.shape, F32)]
    return call(
        onward_kernel, token, [from_down, from_up, meta],
        [
            pl.BlockSpec((rows, cut), lambda j: (0, 0)),
            pl.BlockSpec((rows, width), lambda j: (0, 0)),
            pl.BlockSpec(meta.shape, lambda j: (0, 0)),
        ],
        [jax.ShapeDtypeStruct(*sh) for sh in shapes],
        [pl.BlockSpec(sh[0], lambda j: (0, 0)) for sh in shapes], (1,), 1000,
    )


def prepare_kernel(scalars, saved, saved0, saved0_t, near, near_t, distant, distant_t):
    row = lax.broadcasted_iota(I32, (320, 1), 0)
    source = lax.broadcasted_iota(I32, (320, 1280), 1)
    for q in range(4):
        at = row + q * 320
        plane, line = at // 40, at % 40
        z = jnp.where(line < 32, line // 8, (line - 32) // 2)
        place = jnp.where(line < 32, line % 8, 8 + line % 2)
        hit = (source == z * 320 + plane * CAP + place).astype(F32).astype(BF)
        rows = dot(hit, saved[0])
        saved0[q * 320 : q * 320 + 320, :] = rows.astype(BF)
    saved0_t[...] = saved0[...].astype(F32).T.astype(BF)
    for at, step in enumerate(STEPS):
        begin = pl.multiple_of(((scalars[0] + 4 - step) & 3) * 320, 320)
        rows = saved[1, pl.ds(begin, 320), :]
        if at < 3:
            near[at * 320 : at * 320 + 320, :] = rows
        else:
            distant[...] = rows
    near_t[...] = near[...].astype(F32).T.astype(BF)
    distant_t[...] = distant[...].astype(F32).T.astype(BF)


def prepare(token, scalars, saved):
    _, rows, hidden = saved.shape
    shapes = [(n, hidden)[::turn] for n in (rows, rows * 3 // 4, rows // 4) for turn in (1, -1)]
    return call(
        prepare_kernel, token, [saved], [pl.BlockSpec(saved.shape, lambda j, s: (0, 0, 0))],
        [jax.ShapeDtypeStruct(sh, BF) for sh in shapes],
        [pl.BlockSpec(sh, lambda j, s: (0, 0)) for sh in shapes],
        (1,), 0.1, scalars=scalars,
    )


def picked(meta, rows_of, rows):
    routes, places = positions(meta)
    total = jnp.zeros((rows, meta.shape[1]), F32)
    wanted = lax.broadcasted_iota(I32, total.shape, 0)
    for k in range(TOP):
        row = rows_of(routes[k], places[k])
        total = total + jnp.where(wanted == row, meta[TOP + k : TOP + k + 1, :], 0.0)
    return total.astype(BF), routes, places


def first_pick_kernel(
    scalars, routes, gates, routes_other, gates_other, tokens, tokens_other, out, table, meta, matrix
):
    core = scalars[2]
    count = meta.shape[1]

    @pl.when(pl.program_id(0) == 0)
    def _():
        for s, pair in enumerate(((routes, gates), (routes_other, gates_other))):
            both = jnp.concatenate([x[...].astype(F32) for x in pair], axis=0)
            source = core if s == 0 else 1 - core

            def rows_of(r, place):
                row = ((r >> 2) & 15) * 40 + (r >> 6) * 20 + source * CAP + place
                return jnp.where((r & 3) == 2 * core + 1, row, -1)

            picks, named, places = picked(both, rows_of, out.shape[0])
            matrix[:, s * count : (s + 1) * count] = picks
            if s == 0:
                meta[...] = both
                for k in range(TOP):
                    r = named[k]
                    device = ((r >> 1) & 31) * 4 + (r >> 6) * 2
                    table[k : k + 1, :] = (device + (r & 1)) * CAP + places[k]

    lines = jnp.concatenate([tokens[...], tokens_other[...]], axis=0)
    out[...] = dot(matrix[...], lines).astype(BF)


def first_pick(scalars, slots, slots_other, tokens, tokens_other):
    count, width = tokens.shape
    wide = width // 4
    small = [*slots, *slots_other]
    shapes = [((640, width), BF), ((TOP, count), I32), ((2 * TOP, count), F32)]
    return call(
        first_pick_kernel, None, [*small, tokens, tokens_other],
        [pl.BlockSpec(x.shape, lambda j, s: (0, 0)) for x in small]
        + [pl.BlockSpec((count, wide), lambda j, s: (0, j))] * 2,
        [jax.ShapeDtypeStruct(*sh) for sh in shapes],
        [pl.BlockSpec((640, wide), lambda j, s: (0, j))]
        + [pl.BlockSpec(sh[0], lambda j, s: (0, 0)) for sh in shapes[1:]],
        (4,), 0.1, scratch=[pltpu.VMEM((640, 2 * count), BF)], scalars=scalars,
    )


def line_picker_kernel(scalars, *refs):
    metas, (first, last) = refs[:4], refs[4:]
    count = metas[0].shape[1]
    for s in range(4):
        source = (scalars[0] + 4 - s) & 3

        def rows_of(r, place, low, high, at):
            mine = ((r >> 6) == scalars[1]) & ((r & 1) == 0) & (place >= low) & (place < high)
            return jnp.where(mine, ((r >> 1) & 31) * 8 + at + place - low, -1)

        meta = metas[s][...]
        routes, places = positions(meta)
        wanted = lax.broadcasted_iota(I32, (256, count), 0)
        for out, low, high, at in ((first, 0, 8, 0), (last, 8, CAP, source * 2)):
            total = jnp.zeros((256, count), F32)
            for k in range(TOP):
                row = rows_of(routes[k], places[k], low, high, at)
                total = total + jnp.where(wanted == row, meta[TOP + k : TOP + k + 1, :], 0.0)
            out[:, s * count : (s + 1) * count] = total.astype(BF)


def line_picker(token, scalars, metas):
    count = metas[0].shape[1]
    shape = (256, 4 * count)
    return call(
        line_picker_kernel, token, metas,
        [pl.BlockSpec(x.shape, lambda j, s: (0, 0)) for x in metas],
        [jax.ShapeDtypeStruct(shape, BF)] * 2, [pl.BlockSpec(shape, lambda j, s: (0, 0))] * 2,
        (1,), 0.1, scalars=scalars,
    )


def line_pick_kernel(scalars, first, last, here, down, far_left, far_right, up, out):
    count = here.shape[0]
    left = pl.program_id(0) < pl.num_programs(0) // 2
    far = jnp.where(left, far_left[...], far_right[...])
    tokens = [here[...], down[...], far, up[...]]

    def grouped(rows):
        return rows.reshape(32, 8, rows.shape[1]).astype(BF)

    for s in range(4):
        source = (scalars[0] + 4 - s) & 3
        out[:, source] = grouped(dot(first[:, s * count : (s + 1) * count], tokens[s]))
    out[:, 4] = grouped(dot(last[...], jnp.concatenate(tokens, axis=0)))


def line_pick(token, scalars, matrices, here, down, far, up, block):
    count, width = here.shape
    half = width // block // 2
    every = pl.BlockSpec((count, block), lambda j, s: (0, j))
    (out,), token = call(
        line_pick_kernel, token, [*matrices, here, down, *far, up],
        [pl.BlockSpec(m.shape, lambda j, s: (0, 0)) for m in matrices]
        + [
            every, every,
            pl.BlockSpec((count, block), lambda j, s: (0, jnp.minimum(j, half - 1))),
            pl.BlockSpec((count, block), lambda j, s: (0, jnp.maximum(j - half, 0))),
            every,
        ],
        [jax.ShapeDtypeStruct((32, 5, 8, width), BF)],
        [pl.BlockSpec((32, 5, 8, block), lambda j, s: (0, 0, 0, j))],
        (2 * half,), 0.1, scalars=scalars,
    )
    return out, token


def part_kernel(other, scalars, got, out, *refs):
    picker = refs[-1]
    layer = 1 - scalars[1] if other else scalars[1]

    @pl.when(pl.program_id(0) == 0)
    def _():
        row = lax.broadcasted_iota(I32, (160, 1), 0)
        source = lax.broadcasted_iota(I32, (160, 320), 1)
        picker[...] = (source == row + (row // 20 + layer) * 20).astype(F32).astype(BF)

    for half in range(2):
        rows = dot(picker[...], got[half * 320 : half * 320 + 320, :])
        out[half * 160 : half * 160 + 160, :] = rows.astype(BF)
    if not other:
        left, right = refs[:2]
        wide, rest = out.shape[1], right.shape[1]

        @pl.when(pl.program_id(0) == 0)
        def _():
            left[:, :wide] = out[...]

        @pl.when(pl.program_id(0) == 1)
        def _():
            left[:, wide:] = out[:, : wide - rest]
            right[...] = out[:, wide - rest :]


def part(token, scalars, got, other):
    width = got.shape[1]
    wide = width // 2
    shapes = [(320, width)] + [(320, width * n // 4) for n in (3, 1)] * (not other)
    return call(
        functools.partial(part_kernel, other), token, [got],
        [pl.BlockSpec((640, wide), lambda j, s: (0, j))],
        [jax.ShapeDtypeStruct(sh, BF) for sh in shapes],
        [pl.BlockSpec((320, wide), lambda j, s: (0, j))]
        + [pl.BlockSpec(sh, lambda j, s: (0, 0)) for sh in shapes[1:]],
        (2,), 0.1, scratch=[pltpu.VMEM((160, 320), BF)], scalars=scalars,
        limit=60 if other else LATE,
    )


def hold(token, carried, after):
    anywhere = [pl.BlockSpec(memory_space=pl.ANY)] * len(carried)
    return call(
        lambda *refs: None, token, carried, anywhere,
        [jax.ShapeDtypeStruct(x.shape, x.dtype) for x in carried], anywhere, (1,), 0.1,
        aliases={n: n for n in range(len(carried))}, after=after, limit=LATE,
    )


def lines_of(rows):
    return jnp.concatenate([r[...] for r in rows], axis=0)


def line_specs(rows, wide):
    return [pl.BlockSpec((r.shape[0], wide), lambda j: (0, j)) for r in rows]


def close(total, saved, hidden, terms):
    hidden[...] = total[...].astype(BF)
    products = saved[...].astype(F32) * total[...]
    lanes = sum(products[:, at : at + 128] for at in range(0, products.shape[1], 128))
    terms[...] = jnp.sum(lanes.T, axis=0, keepdims=True)


def back_kernel(pieces, *refs):
    rows, (weight, saved, hidden, terms, total) = refs[:pieces], refs[pieces:]

    @pl.when(pl.program_id(0) == 0)
    def _():
        total[...] = jnp.zeros_like(total)

    total[...] += lax.dot_general(
        lines_of(rows), weight[...], (((1,), (1,)), ((), ())), preferred_element_type=F32
    )
    pl.when(pl.program_id(0) == 1)(functools.partial(close, total, saved, hidden, terms))


def back(token, rows, weight, saved, expert):
    shape = saved.shape
    wide = weight.shape[2] // 2
    whole = pl.BlockSpec(shape, lambda j: (0, 0))
    return call(
        functools.partial(back_kernel, len(rows)), token, [*rows, weight, saved],
        line_specs(rows, wide)
        + [pl.BlockSpec((None, shape[1], wide), lambda j: (expert, 0, j)), whole],
        [jax.ShapeDtypeStruct(shape, BF), jax.ShapeDtypeStruct((1, shape[0]), F32)],
        [whole, pl.BlockSpec((1, shape[0]), lambda j: (0, 0))],
        (2,), 0.1, limit=LATE, scratch=[pltpu.VMEM(shape, F32)],
    )


def down_kernel(pieces, saved_t, *refs):
    refs[pieces][...] = dot(saved_t[...], lines_of(refs[:pieces]))


def down(token, saved_t, rows, width):
    hidden = saved_t.shape[0]
    wide = width // 2
    (out,), token = call(
        functools.partial(down_kernel, len(rows)), token, [saved_t, *rows],
        [pl.BlockSpec(saved_t.shape, lambda j: (0, 0)), *line_specs(rows, wide)],
        [jax.ShapeDtypeStruct((hidden, width), F32)],
        [pl.BlockSpec((hidden, wide), lambda j: (0, j))], (2,), 0.1, limit=LATE,
    )
    return out, token


def distant_kernel(last, rows, weight, saved_t, before, *refs):
    if last:
        so_far, saved, _, out, hidden, terms, total = refs
    else:
        out, total = refs
    out[...] = (dot(saved_t[...], rows[...]) + before[...]).astype(BF)

    @pl.when(pl.program_id(0) == 0)
    def _():
        total[...] = so_far[...] if last else jnp.zeros_like(total)

    total[...] += lax.dot_general(
        rows[...], weight[...], (((1,), (1,)), ((), ())), preferred_element_type=F32
    )
    if last:
        close(total, saved, hidden, terms)


def distant_rows(token, rows, weight, saved, saved_t, before, earlier=None):
    (hidden, width), size = before.shape, rows.shape[0]
    block = width // 4
    last = earlier is not None
    side = 3 * last
    whole = pl.BlockSpec(saved.shape, lambda j: (0, 0))
    out = jax.ShapeDtypeStruct((2, hidden, width), BF)
    total = jax.ShapeDtypeStruct(saved.shape, F32)
    args = [rows, weight, saved_t, before]
    specs = [
        pl.BlockSpec((size, block), lambda j: (0, j)),
        pl.BlockSpec((None, hidden, block), lambda j: (1, 0, j + side)),
        pl.BlockSpec(saved_t.shape, lambda j: (0, 0)),
        pl.BlockSpec((hidden, block), lambda j: (0, j + side)),
    ]
    out_specs = [pl.BlockSpec((None, hidden, block), lambda j: (1, 0, j + side))]
    if last:
        args += [earlier[1], saved, earlier[0]]
        specs += [whole, whole, pl.BlockSpec(memory_space=pl.ANY)]
        shapes = [out, jax.ShapeDtypeStruct(saved.shape, BF), jax.ShapeDtypeStruct((1, size), F32)]
        out_specs += [whole, pl.BlockSpec((1, size), lambda j: (0, 0))]
    else:
        shapes = [out, total]
        out_specs.append(whole)
    return call(
        functools.partial(distant_kernel, last), token, args, specs, shapes, out_specs,
        (rows.shape[1] // block,), 0.1, limit=LATE, scratch=[pltpu.VMEM(saved.shape, F32)] if last else [],
        aliases={6: 0} if last else {},
    )


def finish_kernel(scalars, saved_t, rows, hidden0, near, distant, _, down_out, hidden_out):
    down_out[...] = dot(saved_t[...], rows[...]).astype(BF)
    row = lax.broadcasted_iota(I32, (160, 1), 0)
    plane, place = row // CAP, row % CAP
    source = lax.broadcasted_iota(I32, (160, 640), 1)
    for side in range(2):
        z = 2 * pl.program_id(0) + side
        step = (scalars[0] + 4 - z) & 3
        begin = pl.multiple_of(jnp.where(step == 3, 2, step & 1) * 320, 320)
        hidden_out[1, side * 320 : side * 320 + 320, :] = jnp.where(
            step == 2, distant[...], near[pl.ds(begin, 320), :]
        )
        line = jnp.where(place < 8, z * 8 + place, 24 + z * 2 + place)
        hit = (source == plane * 40 + line).astype(F32).astype(BF)
        for half in range(2):
            lines = dot(hit, hidden0[half * 640 : half * 640 + 640, :])
            at = side * 320 + half * 160
            hidden_out[0, at : at + 160, :] = lines.astype(BF)


def finish(token, scalars, saved_t, rows, hidden0, near, distant, result):
    count, width = rows.shape
    hidden = saved_t.shape[0]
    wide = width // 2
    args = [saved_t, rows, hidden0, near, distant, result]
    specs = [pl.BlockSpec(x.shape, lambda j, s: (0, 0)) for x in args[:-1]]
    specs[1] = pl.BlockSpec((count, wide), lambda j, s: (0, j))
    shape = (2, count, hidden)
    outs, _ = call(
        finish_kernel, token, args, [*specs, pl.BlockSpec(memory_space=pl.ANY)],
        [jax.ShapeDtypeStruct(result.shape, BF), jax.ShapeDtypeStruct(shape, BF)],
        [
            pl.BlockSpec((None, hidden, wide), lambda j, s: (0, 0, j)),
            pl.BlockSpec((2, count // 2, hidden), lambda j, s: (0, j, 0)),
        ],
        (2,), 0.1, scalars=scalars, aliases={len(args): 0},
    )
    return outs


def shards(grad_out, gates, routes, w_down, saved_hidden):
    tokens, width = grad_out.shape
    zh, zl = lax.axis_index("zh"), lax.axis_index("zl")
    core = lax.axis_index("core")
    z = zh * 2 + zl
    scalars = jnp.stack([z, zl, core]).astype(I32)

    wide = width // 2

    from_down, from_up = z_shift(grad_out, 1), z_shift(grad_out, -1)
    slots = (routes.T, gates.T)
    other = core_swap(grad_out)
    (send1, table, meta), token = first_pick(
        scalars, slots, [core_swap(x) for x in slots], grad_out, other
    )
    got1 = lax.all_to_all(send1.reshape(16, 40, width), ("y", "x"), 0, 0, tiled=True)
    got1 = got1.reshape(640, width)

    (onward_down, onward_up, meta), token = onward(token, from_down, from_up, meta, wide)
    metas = [meta, z_shift(meta, 1), z_shift(meta, 2), z_shift(meta, -1)]
    far = (z_shift(onward_down, 1), z_shift(onward_up, -1))
    saved, token = prepare(token, scalars, saved_hidden)
    saved0, saved0_t, saved_near, saved_near_t, saved_distant, saved_distant_t = saved
    matrices, token = line_picker(token, scalars, metas)

    send0, token = line_pick(
        token, scalars, matrices, grad_out, from_down, far, from_up, width // 4
    )
    (away,), token = part(token, scalars, got1, True)
    rows0 = lax.all_to_all(send0, PLANE, 0, 0, tiled=True).reshape(1280, width)
    near = [z_shift(away, 1), z_shift(away, -1)]
    (own, *own_parts), token = part(token, scalars, got1, False)
    own_parts, token = hold(token, own_parts, near)
    near = [own, *near]
    distant = [z_shift(x, 2) for x in own_parts]

    (hidden_near, terms_near), token = back(token, near, w_down, saved_near, 1)
    before, token = down(token, saved_near_t, near, width)
    more = (w_down, saved_distant, saved_distant_t, before)
    earlier, token = distant_rows(token, distant[0], *more)
    (d_down, hidden_distant, terms_distant), token = distant_rows(
        token, distant[1], *more, earlier
    )
    (hidden0, terms0), token = back(token, [rows0], w_down, saved0, 0)
    d_down, d_hidden = finish(
        token, scalars, saved0_t, rows0, hidden0, hidden_near, hidden_distant, d_down
    )

    terms_near = terms_near.reshape(3, 32, CAP)
    terms1 = jnp.stack(
        [terms_near[0], terms_near[1], terms_distant.reshape(32, CAP), terms_near[2]], axis=1
    )
    terms1 = jnp.concatenate(
        [lax.dynamic_index_in_dim(terms1, (z - i) % 4, 1, True) for i in range(4)], axis=1
    )
    terms0 = terms0.reshape(32, 40)
    terms0 = jnp.concatenate(
        [terms0[:, :32].reshape(32, 4, 8), terms0[:, 32:].reshape(32, 4, 2)], axis=2
    )
    terms = jnp.concatenate([terms0, terms1], axis=2).reshape(128, 2 * CAP)
    returned = lax.all_to_all(terms, PLANE + Z, 0, 0, tiled=True)
    returned = returned.reshape(32, 2, 2, 2 * CAP)
    returned = (returned[:, 0] + returned[:, 1]).reshape(-1)

    table = table.reshape(1, -1)
    d_gates = jnp.sum(
        jnp.where(
            table == jnp.arange(EXPERTS * CAP, dtype=I32)[:, None], returned[:, None], 0.0
        ),
        axis=0,
    ).reshape(TOP, tokens).T
    return d_gates / gates.astype(F32), d_down, d_hidden


def solution(mesh):
    fine = Mesh(mesh.devices.reshape(2, 2, 4, 4, 2), ALL)
    in_specs = (
        P(ALL, None),
        P(ALL, None),
        P(ALL, None),
        P(("zl", "y", "x", "core"), "zh", None),
        P(("zl", "y", "x", "core"), None, "zh"),
    )
    out_specs = (P(ALL, None), in_specs[3], in_specs[4])
    return jax.shard_map(shards, mesh=fine, in_specs=in_specs, out_specs=out_specs, check_vma=False)
```

```python
import functools

import jax
import jax.numpy as jnp
from jax import lax
from jax.experimental import pallas as pl
from jax.experimental.pallas import tpu as pltpu
from jax.sharding import Mesh, PartitionSpec as P

Z = ("zh", "zl")
PLANE = ("y", "x", "core")
ALL = ("zh", "zl", "y", "x", "core")
CAP = 10
LATE = 46
TOP = 4
STEPS = (0, 1, 3, 2)
EXPERTS = 128
BF = jnp.bfloat16
F32 = jnp.float32
I32 = jnp.int32


def z_shift(value, step):
    return lax.ppermute(value, Z, [(i, (i + step) % 4) for i in range(4)])


def core_swap(value):
    return lax.ppermute(value, "core", [(0, 1), (1, 0)])


def dot(a, b):
    return jnp.dot(a, b, preferred_element_type=F32)


def call(body, token, args, in_specs, out_shape, out_specs, grid, micros, scratch=(), aliases=None,
         scalars=None, after=(), limit=60):
    lead = 0 if scalars is None else 1
    extra = [*([] if token is None else [token]), *after]
    n_in, n_out = lead + len(args), len(out_shape)

    def run(*refs):
        outs = refs[n_in + len(extra) :]
        outs[n_out][...] = jnp.zeros((8, 128), F32)
        body(*refs[:n_in], *outs[:n_out], *outs[n_out + 1 :])

    result = pl.pallas_call(
        run,
        out_shape=[*out_shape, jax.ShapeDtypeStruct((8, 128), F32)],
        grid_spec=pltpu.PrefetchScalarGridSpec(
            num_scalar_prefetch=lead,
            grid=grid,
            in_specs=[*in_specs, *[pl.BlockSpec(memory_space=pl.ANY)] * len(extra)],
            out_specs=[*out_specs, pl.BlockSpec((8, 128), lambda j, *_: (0, 0))],
            scratch_shapes=list(scratch),
        ),
        input_output_aliases=aliases or {},
        compiler_params=pltpu.CompilerParams(vmem_limit_bytes=limit * 1024 * 1024),
        cost_estimate=pl.CostEstimate(
            flops=int(micros * 1e9), bytes_accessed=0, transcendentals=0
        ),
    )(*([] if scalars is None else [scalars]), *args, *extra)
    return result[:-1], result[-1]


def positions(meta):
    tokens = meta.shape[1]
    names = lax.broadcasted_iota(I32, (EXPERTS, tokens), 0)
    routes = [meta[k : k + 1, :].astype(I32) for k in range(TOP)]
    hits = [names == r for r in routes]
    named = sum(h.astype(F32) for h in hits)
    first = lax.broadcasted_iota(I32, (tokens, tokens), 0)
    second = lax.broadcasted_iota(I32, (tokens, tokens), 1)
    earlier = dot(named.astype(BF), (first < second).astype(F32).astype(BF))
    places = [
        jnp.sum(jnp.where(h, earlier, 0.0), axis=0, keepdims=True).astype(I32) for h in hits
    ]
    return routes, places


def onward_kernel(below, above, meta, down, up, meta_out):
    cut = down.shape[1]
    down[...] = below[:, :cut]
    up[...] = above[:, cut:]
    meta_out[...] = meta[...]


def onward(token, from_down, from_up, meta, cut):
    rows, width = from_down.shape
    shapes = [((rows, cut), BF), ((rows, width - cut), BF), (meta.shape, F32)]
    return call(
        onward_kernel, token, [from_down, from_up, meta],
        [
            pl.BlockSpec((rows, cut), lambda j: (0, 0)),
            pl.BlockSpec((rows, width), lambda j: (0, 0)),
            pl.BlockSpec(meta.shape, lambda j: (0, 0)),
        ],
        [jax.ShapeDtypeStruct(*sh) for sh in shapes],
        [pl.BlockSpec(sh[0], lambda j: (0, 0)) for sh in shapes], (1,), 1000,
    )


def prepare_kernel(scalars, saved, saved0, saved0_t, near, near_t, distant, distant_t):
    row = lax.broadcasted_iota(I32, (320, 1), 0)
    source = lax.broadcasted_iota(I32, (320, 1280), 1)
    for q in range(4):
        at = row + q * 320
        plane, line = at // 40, at % 40
        z = jnp.where(line < 32, line // 8, (line - 32) // 2)
        place = jnp.where(line < 32, line % 8, 8 + line % 2)
        hit = (source == z * 320 + plane * CAP + place).astype(F32).astype(BF)
        rows = dot(hit, saved[0])
        saved0[q * 320 : q * 320 + 320, :] = rows.astype(BF)
    saved0_t[...] = saved0[...].astype(F32).T.astype(BF)
    for at, step in enumerate(STEPS):
        begin = pl.multiple_of(((scalars[0] + 4 - step) & 3) * 320, 320)
        rows = saved[1, pl.ds(begin, 320), :]
        if at < 3:
            near[at * 320 : at * 320 + 320, :] = rows
        else:
            distant[...] = rows
    near_t[...] = near[...].astype(F32).T.astype(BF)
    distant_t[...] = distant[...].astype(F32).T.astype(BF)


def prepare(token, scalars, saved):
    _, rows, hidden = saved.shape
    shapes = [(n, hidden)[::turn] for n in (rows, rows * 3 // 4, rows // 4) for turn in (1, -1)]
    return call(
        prepare_kernel, token, [saved], [pl.BlockSpec(saved.shape, lambda j, s: (0, 0, 0))],
        [jax.ShapeDtypeStruct(sh, BF) for sh in shapes],
        [pl.BlockSpec(sh, lambda j, s: (0, 0)) for sh in shapes],
        (1,), 0.1, scalars=scalars,
    )


def picked(meta, rows_of, rows):
    routes, places = positions(meta)
    total = jnp.zeros((rows, meta.shape[1]), F32)
    wanted = lax.broadcasted_iota(I32, total.shape, 0)
    for k in range(TOP):
        row = rows_of(routes[k], places[k])
        total = total + jnp.where(wanted == row, meta[TOP + k : TOP + k + 1, :], 0.0)
    return total.astype(BF), routes, places


def first_pick_kernel(
    scalars, routes, gates, routes_other, gates_other, tokens, tokens_other, out, table, meta, matrix
):
    core = scalars[2]
    count = meta.shape[1]

    @pl.when(pl.program_id(0) == 0)
    def _():
        for s, pair in enumerate(((routes, gates), (routes_other, gates_other))):
            both = jnp.concatenate([x[...].astype(F32) for x in pair], axis=0)
            source = core if s == 0 else 1 - core

            def rows_of(r, place):
                row = ((r >> 2) & 15) * 40 + (r >> 6) * 20 + source * CAP + place
                return jnp.where((r & 3) == 2 * core + 1, row, -1)

            picks, named, places = picked(both, rows_of, out.shape[0])
            matrix[:, s * count : (s + 1) * count] = picks
            if s == 0:
                meta[...] = both
                for k in range(TOP):
                    r = named[k]
                    device = ((r >> 1) & 31) * 4 + (r >> 6) * 2
                    table[k : k + 1, :] = (device + (r & 1)) * CAP + places[k]

    lines = jnp.concatenate([tokens[...], tokens_other[...]], axis=0)
    out[...] = dot(matrix[...], lines).astype(BF)


def first_pick(scalars, slots, slots_other, tokens, tokens_other):
    count, width = tokens.shape
    wide = width // 2
    small = [*slots, *slots_other]
    shapes = [((640, width), BF), ((TOP, count), I32), ((2 * TOP, count), F32)]
    return call(
        first_pick_kernel, None, [*small, tokens, tokens_other],
        [pl.BlockSpec(x.shape, lambda j, s: (0, 0)) for x in small]
        + [pl.BlockSpec((count, wide), lambda j, s: (0, j))] * 2,
        [jax.ShapeDtypeStruct(*sh) for sh in shapes],
        [pl.BlockSpec((640, wide), lambda j, s: (0, j))]
        + [pl.BlockSpec(sh[0], lambda j, s: (0, 0)) for sh in shapes[1:]],
        (2,), 0.1, scratch=[pltpu.VMEM((640, 2 * count), BF)], scalars=scalars,
    )


def line_picker_kernel(scalars, *refs):
    metas, (first, last) = refs[:4], refs[4:]
    count = metas[0].shape[1]
    for s in range(4):
        source = (scalars[0] + 4 - s) & 3

        def rows_of(r, place, low, high, at):
            mine = ((r >> 6) == scalars[1]) & ((r & 1) == 0) & (place >= low) & (place < high)
            return jnp.where(mine, ((r >> 1) & 31) * 8 + at + place - low, -1)

        meta = metas[s][...]
        routes, places = positions(meta)
        wanted = lax.broadcasted_iota(I32, (256, count), 0)
        for out, low, high, at in ((first, 0, 8, 0), (last, 8, CAP, source * 2)):
            total = jnp.zeros((256, count), F32)
            for k in range(TOP):
                row = rows_of(routes[k], places[k], low, high, at)
                total = total + jnp.where(wanted == row, meta[TOP + k : TOP + k + 1, :], 0.0)
            out[:, s * count : (s + 1) * count] = total.astype(BF)


def line_picker(token, scalars, metas):
    count = metas[0].shape[1]
    shape = (256, 4 * count)
    return call(
        line_picker_kernel, token, metas,
        [pl.BlockSpec(x.shape, lambda j, s: (0, 0)) for x in metas],
        [jax.ShapeDtypeStruct(shape, BF)] * 2, [pl.BlockSpec(shape, lambda j, s: (0, 0))] * 2,
        (1,), 0.1, scalars=scalars,
    )


def line_pick_kernel(scalars, first, last, here, down, far_left, far_right, up, out):
    count = here.shape[0]
    left = pl.program_id(0) < pl.num_programs(0) // 2
    far = jnp.where(left, far_left[...], far_right[...])
    tokens = [here[...], down[...], far, up[...]]

    def grouped(rows):
        return rows.reshape(32, 8, rows.shape[1]).astype(BF)

    for s in range(4):
        source = (scalars[0] + 4 - s) & 3
        out[:, source] = grouped(dot(first[:, s * count : (s + 1) * count], tokens[s]))
    out[:, 4] = grouped(dot(last[...], jnp.concatenate(tokens, axis=0)))


def line_pick(token, scalars, matrices, here, down, far, up, block):
    count, width = here.shape
    half = width // block // 2
    every = pl.BlockSpec((count, block), lambda j, s: (0, j))
    (out,), token = call(
        line_pick_kernel, token, [*matrices, here, down, *far, up],
        [pl.BlockSpec(m.shape, lambda j, s: (0, 0)) for m in matrices]
        + [
            every, every,
            pl.BlockSpec((count, block), lambda j, s: (0, jnp.minimum(j, half - 1))),
            pl.BlockSpec((count, block), lambda j, s: (0, jnp.maximum(j - half, 0))),
            every,
        ],
        [jax.ShapeDtypeStruct((32, 5, 8, width), BF)],
        [pl.BlockSpec((32, 5, 8, block), lambda j, s: (0, 0, 0, j))],
        (2 * half,), 0.1, scalars=scalars,
    )
    return out, token


def part_kernel(other, scalars, got, out, *refs):
    picker = refs[-1]
    layer = 1 - scalars[1] if other else scalars[1]

    @pl.when(pl.program_id(0) == 0)
    def _():
        row = lax.broadcasted_iota(I32, (160, 1), 0)
        source = lax.broadcasted_iota(I32, (160, 320), 1)
        picker[...] = (source == row + (row // 20 + layer) * 20).astype(F32).astype(BF)

    for half in range(2):
        rows = dot(picker[...], got[half * 320 : half * 320 + 320, :])
        out[half * 160 : half * 160 + 160, :] = rows.astype(BF)
    if not other:
        left, right = refs[:2]
        wide, rest = out.shape[1], right.shape[1]

        @pl.when(pl.program_id(0) == 0)
        def _():
            left[:, :wide] = out[...]

        @pl.when(pl.program_id(0) == 1)
        def _():
            left[:, wide:] = out[:, : wide - rest]
            right[...] = out[:, wide - rest :]


def part(token, scalars, got, other):
    width = got.shape[1]
    wide = width // 2
    shapes = [(320, width)] + [(320, width * n // 4) for n in (3, 1)] * (not other)
    return call(
        functools.partial(part_kernel, other), token, [got],
        [pl.BlockSpec((640, wide), lambda j, s: (0, j))],
        [jax.ShapeDtypeStruct(sh, BF) for sh in shapes],
        [pl.BlockSpec((320, wide), lambda j, s: (0, j))]
        + [pl.BlockSpec(sh, lambda j, s: (0, 0)) for sh in shapes[1:]],
        (2,), 0.1, scratch=[pltpu.VMEM((160, 320), BF)], scalars=scalars,
        limit=60 if other else LATE,
    )


def hold(token, carried, after):
    anywhere = [pl.BlockSpec(memory_space=pl.ANY)] * len(carried)
    return call(
        lambda *refs: None, token, carried, anywhere,
        [jax.ShapeDtypeStruct(x.shape, x.dtype) for x in carried], anywhere, (1,), 0.1,
        aliases={n: n for n in range(len(carried))}, after=after, limit=LATE,
    )


def lines_of(rows):
    return jnp.concatenate([r[...] for r in rows], axis=0)


def line_specs(rows, wide):
    return [pl.BlockSpec((r.shape[0], wide), lambda j: (0, j)) for r in rows]


def close(total, saved, hidden, terms):
    hidden[...] = total[...].astype(BF)
    products = saved[...].astype(F32) * total[...]
    lanes = sum(products[:, at : at + 128] for at in range(0, products.shape[1], 128))
    terms[...] = jnp.sum(lanes.T, axis=0, keepdims=True)


def back_kernel(pieces, *refs):
    rows, (weight, saved, hidden, terms, total) = refs[:pieces], refs[pieces:]

    @pl.when(pl.program_id(0) == 0)
    def _():
        total[...] = jnp.zeros_like(total)

    total[...] += lax.dot_general(
        lines_of(rows), weight[...], (((1,), (1,)), ((), ())), preferred_element_type=F32
    )
    pl.when(pl.program_id(0) == 1)(functools.partial(close, total, saved, hidden, terms))


def back(token, rows, weight, saved, expert):
    shape = saved.shape
    wide = weight.shape[2] // 2
    whole = pl.BlockSpec(shape, lambda j: (0, 0))
    return call(
        functools.partial(back_kernel, len(rows)), token, [*rows, weight, saved],
        line_specs(rows, wide)
        + [pl.BlockSpec((None, shape[1], wide), lambda j: (expert, 0, j)), whole],
        [jax.ShapeDtypeStruct(shape, BF), jax.ShapeDtypeStruct((1, shape[0]), F32)],
        [whole, pl.BlockSpec((1, shape[0]), lambda j: (0, 0))],
        (2,), 0.1, limit=LATE, scratch=[pltpu.VMEM(shape, F32)],
    )


def down_kernel(pieces, saved_t, *refs):
    refs[pieces][...] = dot(saved_t[...], lines_of(refs[:pieces]))


def down(token, saved_t, rows, width):
    hidden = saved_t.shape[0]
    wide = width // 2
    (out,), token = call(
        functools.partial(down_kernel, len(rows)), token, [saved_t, *rows],
        [pl.BlockSpec(saved_t.shape, lambda j: (0, 0)), *line_specs(rows, wide)],
        [jax.ShapeDtypeStruct((hidden, width), F32)],
        [pl.BlockSpec((hidden, wide), lambda j: (0, j))], (2,), 0.1, limit=LATE,
    )
    return out, token


def distant_kernel(last, rows, weight, saved_t, before, *refs):
    if last:
        so_far, saved, _, out, hidden, terms, total = refs
    else:
        out, total = refs
    out[...] = (dot(saved_t[...], rows[...]) + before[...]).astype(BF)

    @pl.when(pl.program_id(0) == 0)
    def _():
        total[...] = so_far[...] if last else jnp.zeros_like(total)

    total[...] += lax.dot_general(
        rows[...], weight[...], (((1,), (1,)), ((), ())), preferred_element_type=F32
    )
    if last:
        close(total, saved, hidden, terms)


def distant_rows(token, rows, weight, saved, saved_t, before, earlier=None):
    (hidden, width), size = before.shape, rows.shape[0]
    block = width // 4
    last = earlier is not None
    side = 3 * last
    whole = pl.BlockSpec(saved.shape, lambda j: (0, 0))
    out = jax.ShapeDtypeStruct((2, hidden, width), BF)
    total = jax.ShapeDtypeStruct(saved.shape, F32)
    args = [rows, weight, saved_t, before]
    specs = [
        pl.BlockSpec((size, block), lambda j: (0, j)),
        pl.BlockSpec((None, hidden, block), lambda j: (1, 0, j + side)),
        pl.BlockSpec(saved_t.shape, lambda j: (0, 0)),
        pl.BlockSpec((hidden, block), lambda j: (0, j + side)),
    ]
    out_specs = [pl.BlockSpec((None, hidden, block), lambda j: (1, 0, j + side))]
    if last:
        args += [earlier[1], saved, earlier[0]]
        specs += [whole, whole, pl.BlockSpec(memory_space=pl.ANY)]
        shapes = [out, jax.ShapeDtypeStruct(saved.shape, BF), jax.ShapeDtypeStruct((1, size), F32)]
        out_specs += [whole, pl.BlockSpec((1, size), lambda j: (0, 0))]
    else:
        shapes = [out, total]
        out_specs.append(whole)
    return call(
        functools.partial(distant_kernel, last), token, args, specs, shapes, out_specs,
        (rows.shape[1] // block,), 0.1, limit=LATE, scratch=[pltpu.VMEM(saved.shape, F32)] if last else [],
        aliases={6: 0} if last else {},
    )


def finish_kernel(scalars, saved_t, rows, hidden0, near, distant, _, down_out, hidden_out):
    down_out[...] = dot(saved_t[...], rows[...]).astype(BF)
    row = lax.broadcasted_iota(I32, (160, 1), 0)
    plane, place = row // CAP, row % CAP
    source = lax.broadcasted_iota(I32, (160, 640), 1)
    for side in range(2):
        z = 2 * pl.program_id(0) + side
        step = (scalars[0] + 4 - z) & 3
        begin = pl.multiple_of(jnp.where(step == 3, 2, step & 1) * 320, 320)
        hidden_out[1, side * 320 : side * 320 + 320, :] = jnp.where(
            step == 2, distant[...], near[pl.ds(begin, 320), :]
        )
        line = jnp.where(place < 8, z * 8 + place, 24 + z * 2 + place)
        hit = (source == plane * 40 + line).astype(F32).astype(BF)
        for half in range(2):
            lines = dot(hit, hidden0[half * 640 : half * 640 + 640, :])
            at = side * 320 + half * 160
            hidden_out[0, at : at + 160, :] = lines.astype(BF)


def finish(token, scalars, saved_t, rows, hidden0, near, distant, result):
    count, width = rows.shape
    hidden = saved_t.shape[0]
    wide = width // 2
    args = [saved_t, rows, hidden0, near, distant, result]
    specs = [pl.BlockSpec(x.shape, lambda j, s: (0, 0)) for x in args[:-1]]
    specs[1] = pl.BlockSpec((count, wide), lambda j, s: (0, j))
    shape = (2, count, hidden)
    outs, _ = call(
        finish_kernel, token, args, [*specs, pl.BlockSpec(memory_space=pl.ANY)],
        [jax.ShapeDtypeStruct(result.shape, BF), jax.ShapeDtypeStruct(shape, BF)],
        [
            pl.BlockSpec((None, hidden, wide), lambda j, s: (0, 0, j)),
            pl.BlockSpec((2, count // 2, hidden), lambda j, s: (0, j, 0)),
        ],
        (2,), 0.1, scalars=scalars, aliases={len(args): 0},
    )
    return outs


def shards(grad_out, gates, routes, w_down, saved_hidden):
    tokens, width = grad_out.shape
    zh, zl = lax.axis_index("zh"), lax.axis_index("zl")
    core = lax.axis_index("core")
    z = zh * 2 + zl
    scalars = jnp.stack([z, zl, core]).astype(I32)

    wide = width // 2

    from_down, from_up = z_shift(grad_out, 1), z_shift(grad_out, -1)
    slots = (routes.T, gates.T)
    other = core_swap(grad_out)
    (send1, table, meta), token = first_pick(
        scalars, slots, [core_swap(x) for x in slots], grad_out, other
    )
    got1 = lax.all_to_all(send1.reshape(16, 40, width), ("y", "x"), 0, 0, tiled=True)
    got1 = got1.reshape(640, width)

    (onward_down, onward_up, meta), token = onward(token, from_down, from_up, meta, wide)
    metas = [meta, z_shift(meta, 1), z_shift(meta, 2), z_shift(meta, -1)]
    far = (z_shift(onward_down, 1), z_shift(onward_up, -1))
    saved, token = prepare(token, scalars, saved_hidden)
    saved0, saved0_t, saved_near, saved_near_t, saved_distant, saved_distant_t = saved
    matrices, token = line_picker(token, scalars, metas)

    send0, token = line_pick(
        token, scalars, matrices, grad_out, from_down, far, from_up, width // 4
    )
    (away,), token = part(token, scalars, got1, True)
    rows0 = lax.all_to_all(send0, PLANE, 0, 0, tiled=True).reshape(1280, width)
    near = [z_shift(away, 1), z_shift(away, -1)]
    (own, *own_parts), token = part(token, scalars, got1, False)
    own_parts, token = hold(token, own_parts, near)
    near = [own, *near]
    distant = [z_shift(x, 2) for x in own_parts]

    (hidden_near, terms_near), token = back(token, near, w_down, saved_near, 1)
    before, token = down(token, saved_near_t, near, width)
    more = (w_down, saved_distant, saved_distant_t, before)
    earlier, token = distant_rows(token, distant[0], *more)
    (d_down, hidden_distant, terms_distant), token = distant_rows(
        token, distant[1], *more, earlier
    )
    (hidden0, terms0), token = back(token, [rows0], w_down, saved0, 0)
    d_down, d_hidden = finish(
        token, scalars, saved0_t, rows0, hidden0, hidden_near, hidden_distant, d_down
    )

    terms_near = terms_near.reshape(3, 32, CAP)
    terms1 = jnp.stack(
        [terms_near[0], terms_near[1], terms_distant.reshape(32, CAP), terms_near[2]], axis=1
    )
    terms1 = jnp.concatenate(
        [lax.dynamic_index_in_dim(terms1, (z - i) % 4, 1, True) for i in range(4)], axis=1
    )
    terms0 = terms0.reshape(32, 40)
    terms0 = jnp.concatenate(
        [terms0[:, :32].reshape(32, 4, 8), terms0[:, 32:].reshape(32, 4, 2)], axis=2
    )
    terms = jnp.concatenate([terms0, terms1], axis=2).reshape(128, 2 * CAP)
    returned = lax.all_to_all(terms, PLANE + Z, 0, 0, tiled=True)
    returned = returned.reshape(32, 2, 2, 2 * CAP)
    returned = (returned[:, 0] + returned[:, 1]).reshape(-1)

    table = table.reshape(1, -1)
    d_gates = jnp.sum(
        jnp.where(
            table == jnp.arange(EXPERTS * CAP, dtype=I32)[:, None], returned[:, None], 0.0
        ),
        axis=0,
    ).reshape(TOP, tokens).T
    return d_gates / gates.astype(F32), d_down, d_hidden


def solution(mesh):
    fine = Mesh(mesh.devices.reshape(2, 2, 4, 4, 2), ALL)
    in_specs = (
        P(ALL, None),
        P(ALL, None),
        P(ALL, None),
        P(("zl", "y", "x", "core"), "zh", None),
        P(("zl", "y", "x", "core"), None, "zh"),
    )
    out_specs = (P(ALL, None), in_specs[3], in_specs[4])
    return jax.shard_map(shards, mesh=fine, in_specs=in_specs, out_specs=out_specs, check_vma=False)
```
